32 devices in a mesh: slab: 4 (over y, x), row: 2 (over core), col: 4 (over z).
Axes of the slice: x: 2, y: 2, z: 4, core: 2. Of those that a mesh axis runs over, the one named last changes fastest.
Arguments:
- sources: float32 [4, 4, 2, 1536, 256], P('slab', 'col', 'row'), may hold values from -6 to 6
- tr_vals: float32 [4, 4, 2, 24, 12, 128, 128], P('slab', 'col', 'row'), may hold values from -0.09375 to 0.09375
- tr_cols: int32 [4, 4, 2, 24, 12], P('slab', 'col', 'row'), may hold values from 0 to 47, as said below
- rf_vals: float32 [4, 4, 2, 24, 12, 128, 128], P('slab', 'col', 'row'), may hold values from -0.078125 to 0.078125
- rf_cols: int32 [4, 4, 2, 24, 12], P('slab', 'col', 'row'), may hold values from 0 to 47, as said below
Outputs:
- total_traces: float32 [4, 4, 2, 1536, 256], P('slab', 'col', 'row')
The draws below stay inside these ranges and needn't reach their ends.
Inputs may be any that keep to these rules, and one draw needn't show every extreme that they name: `tr_cols`: each block row lists 12 different column blocks of its column group. `rf_cols`: each block row lists 12 different column blocks of its column group.
All inputs are finite; a program needn't handle non-finite values.
Results may differ from the reference program's by a relative error of at most 0.0001.
Values sent between devices are 32-bit elements; how exact they have to be, the bound alone decides.
No kernel may reach another device: no remote copies, remote signals or barrier semaphores. Data moves between devices by JAX's collectives and lax.ppermute only.
A program may use at most 192 MiB of HBM per device.

```python
import jax
import jax.numpy as jnp
from jax import lax

M = 12288
BS = 128
S = 256
SLABS = 4
GC = 4
GR = 2
P_SIZE = 1536
RB = 24
CB = 48
K = 12


def pick_blocks(key):
    scores = jax.random.randint(key, (SLABS, GC, GR, RB, CB), 0, 1 << 20, dtype=jnp.int32)
    scores = scores * CB + jnp.arange(CB, dtype=jnp.int32)
    order = jnp.argsort(scores, axis=-1)[..., :K]
    return order.astype(jnp.int32)


def draw_tr_cols(key, part):
    return pick_blocks(jax.random.fold_in(key, 11))


def draw_rf_cols(key, part):
    return pick_blocks(jax.random.fold_in(key, 23))


def levels(rng, shape, split, smallest, largest):
    factor_of, own = 1.0, jax.random.fold_in(rng, 6)
    for axis_at, parts in split:
        steps = jnp.exp(jax.random.uniform(jax.random.fold_in(own, axis_at), (parts,), jnp.float32, smallest / len(split), largest / len(split)))
        factor_of = factor_of * jnp.repeat(steps, shape[axis_at] // parts).reshape([-1 if axis == axis_at else 1 for axis in range(len(shape))])
    return factor_of


def bell_draw(key, dims, spread, reach, shards=(), kind=jnp.bfloat16):
    level = levels(key, dims, shards, -0.22, 0.18) if shards else 1.0
    entries = jax.random.normal(key, dims, jnp.float32) * spread * level
    return jnp.minimum(jnp.maximum(entries, -reach), reach).astype(kind)


def setup_inputs(seed: int = 0) -> dict:
    key_of = jax.random.split(jax.random.key(seed), 6)
    return {
        "sources": bell_draw(key_of[0], (SLABS, GC, GR, P_SIZE, S), 1.0, 6.0, ((0, 4), (1, 4), (2, 2)), jnp.float32),
        "tr_vals": bell_draw(key_of[1], (SLABS, GC, GR, RB, K, BS, BS), (M // 3) ** -0.5, 0.09375, ((0, 4), (1, 4), (2, 2)), jnp.float32),
        "tr_cols": draw_tr_cols(jax.random.fold_in(key_of[5], 71), 0),
        "rf_vals": bell_draw(key_of[3], (SLABS, GC, GR, RB, K, BS, BS), (M // 2) ** -0.5, 0.078125, ((0, 4), (1, 4), (2, 2)), jnp.float32),
        "rf_cols": draw_rf_cols(jax.random.fold_in(key_of[5], 71), 0),
    }


def apply_operator(values, columns, trace):
    groups_c = columns.shape[0]
    groups_r = columns.shape[1]
    width_cols = trace.shape[3]
    tiles = jnp.transpose(trace, (1, 0, 2, 3)).reshape(groups_r, -1, BS, width_cols)
    which_r = jnp.arange(groups_r, dtype=jnp.int32)[None, :, None, None]
    picked = tiles[which_r, columns]
    summed = jnp.einsum("crikab,crikbs->cias", values, picked, precision=lax.Precision.HIGHEST)
    return summed.reshape(groups_c, groups_r, -1, width_cols)


def reference(sources, tr_vals, tr_cols, rf_vals, rf_cols):
    down_list = []
    refl_list = []
    previous = jnp.zeros(sources.shape[1:], jnp.float32)
    for section in range(SLABS):
        incident = sources[section] + previous
        moved = apply_operator(tr_vals[section], tr_cols[section], incident)
        reflected = apply_operator(rf_vals[section], rf_cols[section], incident)
        down_list.append(moved)
        refl_list.append(reflected)
        previous = moved
    up_list = [None] * SLABS
    above = jnp.zeros(sources.shape[1:], jnp.float32)
    for section in range(SLABS - 1, -1, -1):
        above = apply_operator(tr_vals[section], tr_cols[section], refl_list[section] + above)
        up_list[section] = above
    return jnp.stack(down_list) + jnp.stack(up_list)
```

```python
import functools

import jax
import jax.numpy as jnp
from jax import lax
from jax.experimental import pallas as pl
from jax.experimental.pallas import tpu as pltpu
from jax.sharding import PartitionSpec as P

BATCHES = 8
DELAY = 2


def divisor_up_to(number, limit):
    return max(n for n in range(1, limit + 1) if number % n == 0)


def passed_along(value, axis, steps):
    count = lax.axis_size(axis)
    initial, last = (max(0, -steps), min(count, count - steps))
    return lax.ppermute(value, axis, [(source, source + steps) for source in range(initial, last)])


def split_kernel(values_ref, parts_ref):
    for k in range(values_ref.shape[1]):
        value = values_ref[0, k]
        high = value.astype(jnp.bfloat16)
        size = value.shape[0]
        parts_ref[0, k, :size] = high
        parts_ref[0, k, size:] = (value - high.astype(jnp.float32)).astype(jnp.bfloat16)


def split_operator(values):
    rows, picks, size, depth = values.shape
    return pl.pallas_call(
        split_kernel,
        grid=(rows,),
        in_specs=[pl.BlockSpec((1, picks, size, depth), lambda i: (i, 0, 0, 0))],
        out_specs=pl.BlockSpec((1, picks, 2 * size, depth), lambda i: (i, 0, 0, 0)),
        out_shape=jax.ShapeDtypeStruct((rows, picks, 2 * size, depth), jnp.bfloat16),
        compiler_params=pltpu.CompilerParams(vmem_limit_bytes=24 * 2**20),
        cost_estimate=pl.CostEstimate(flops=0, bytes_accessed=8 * values.size, transcendentals=0),
        name="split_operator",
    )(values)


def apply_kernel(half, index_ref, place_ref, parts_ref, gathered_ref, own_ref, other_ref, tiles):
    step = pl.program_id(0)
    rows, picks, _, size = parts_ref.shape
    pieces, span, piece_rows = gathered_ref.shape
    per_piece = piece_rows // size

    @pl.when(step == 0)
    def _():
        for piece in range(pieces):
            for j in range(per_piece):
                tile = gathered_ref[piece, :, j * size : (j + 1) * size]
                high = tile.astype(jnp.bfloat16).astype(jnp.float32)
                both = jnp.concatenate([high, tile - high], axis=0)
                tiles[piece * per_piece + j] = both.T.astype(jnp.bfloat16)

    place = place_ref[0]
    first = jnp.where(step < half, (1 - place) * half + step, place * half + step - half) * rows
    found = []
    for i in range(rows):
        base = (first + i) * picks
        picked = jnp.concatenate([tiles[index_ref[base + k]] for k in range(picks)], axis=0)
        block = jnp.concatenate([parts_ref[i, k] for k in range(picks)], axis=1)
        product = jnp.dot(block, picked, preferred_element_type=jnp.float32)
        both = (product[:size] + product[size:]).T
        found.append(both[:span] + both[span:])
    result = jnp.concatenate(found, axis=1)

    @pl.when(step < half)
    def _():
        other_ref[...] = result

    @pl.when(step >= half)
    def _():
        own_ref[...] = result


def apply_operator(parts, index, place, gathered):
    block_rows, picks, twice, size = parts.shape
    pieces, span, piece_rows = gathered.shape
    out_rows = block_rows // 2 * size
    rows = divisor_up_to(block_rows // 2, 4)
    half = block_rows // 2 // rows

    def block_of(step, index_ref, place_ref):
        place = place_ref[0]
        return (jnp.where(step < half, (1 - place) * half + step, place * half + step - half), 0, 0, 0)

    spec = pltpu.PrefetchScalarGridSpec(
        num_scalar_prefetch=2,
        grid=(2 * half,),
        in_specs=[
            pl.BlockSpec((rows, picks, twice, size), block_of),
            pl.BlockSpec((pieces, span, piece_rows), lambda step, *_: (0, 0, 0)),
        ],
        out_specs=[
            pl.BlockSpec((span, rows * size), lambda step, *_: (0, jnp.maximum(step - half, 0))),
            pl.BlockSpec((span, rows * size), lambda step, *_: (0, jnp.minimum(step, half - 1))),
        ],
        scratch_shapes=[pltpu.VMEM((pieces * piece_rows // size, size, 2 * span), jnp.bfloat16)],
    )
    return pl.pallas_call(
        functools.partial(apply_kernel, half),
        grid_spec=spec,
        out_shape=[jax.ShapeDtypeStruct((span, out_rows), jnp.float32)] * 2,
        compiler_params=pltpu.CompilerParams(vmem_limit_bytes=32 * 2**20),
        cost_estimate=pl.CostEstimate(
            flops=2 * parts.size * 2 * span,
            bytes_accessed=2 * parts.size + 4 * gathered.size,
            transcendentals=0,
        ),
        name="apply_operator",
    )(index, place, parts, gathered)


def shards(sources, tr_vals, tr_cols, rf_vals, rf_cols):
    source = sources[0, 0, 0]
    piece_rows, columns = source.shape
    batches, delay = BATCHES, DELAY
    span = columns // batches
    length = lax.axis_size("slab")
    position = lax.axis_index("slab")
    place = lax.axis_index("row").reshape(1)
    source = source.T.reshape(batches, span, piece_rows)
    trans = split_operator(tr_vals[0, 0, 0])
    refl = split_operator(rf_vals[0, 0, 0])
    trans_index = tr_cols.reshape(-1)
    refl_index = rf_cols.reshape(-1)
    swap = [(0, 1), (1, 0)]

    def applied(parts, index, gathered):
        own, other = apply_operator(parts, index, place, gathered)
        return own + lax.ppermute(other, "row", swap)

    def batch_at(store, which, start):
        return lax.dynamic_index_in_dim(store, jnp.clip(which, 0, batches - 1) + start, 0, keepdims=False)

    moments = batches + delay * (length - 1)
    zero = jnp.zeros((span, piece_rows), jnp.float32)
    downs, refls, ups = [], [], []
    for moment in range(moments):
        incident = batch_at(source, moment - delay * position, 0)
        if moment >= delay:
            incident = incident + passed_along(downs[moment - delay], "slab", 1)
        gathered = lax.all_gather(incident, "col", axis=0, tiled=False)
        downs.append(applied(trans, trans_index, gathered))
        refls.append(applied(refl, refl_index, gathered))
    reflected = jnp.stack(refls)
    for moment in range(moments):
        incident = batch_at(reflected, moment - delay * (length - 1 - position), delay * position)
        if moment >= delay:
            incident = incident + passed_along(ups[moment - delay], "slab", -1)
        gathered = lax.all_gather(incident, "col", axis=0, tiled=False)
        ups.append(applied(trans, trans_index, gathered))
    down = lax.dynamic_slice_in_dim(jnp.stack(downs), delay * position, batches, 0)
    up = lax.dynamic_slice_in_dim(jnp.stack(ups), delay * (length - 1 - position), batches, 0)
    total = (down + up).reshape(columns, piece_rows).T
    return total[None, None, None]


def solution(mesh):
    placed = (
        P("slab", "col", "row", None, None),
        P("slab", "col", "row", None, None, None, None),
        P("slab", "col", "row", None, None),
        P("slab", "col", "row", None, None, None, None),
        P("slab", "col", "row", None, None),
    )
    return jax.shard_map(
        shards,
        mesh=mesh,
        in_specs=placed,
        out_specs=P("slab", "col", "row", None, None),
        check_vma=False,
    )
```

```python
import jax
import jax.numpy as jnp
from jax import lax
from jax.experimental import pallas as pl
from jax.experimental.pallas import tpu as pltpu
from jax.sharding import PartitionSpec as P

BATCHES = 8
DELAY = 2


def divisor_up_to(number, limit):
    return max(n for n in range(1, limit + 1) if number % n == 0)


def passed_along(value, axis, steps):
    count = lax.axis_size(axis)
    initial, last = (max(0, -steps), min(count, count - steps))
    return lax.ppermute(value, axis, [(source, source + steps) for source in range(initial, last)])


def split_kernel(place_ref, own_ref, other_ref, parts_ref):
    picks, size = own_ref.shape[1:3]

    def split(values_ref, start):
        for k in range(picks):
            value = values_ref[0, k]
            high = value.astype(jnp.bfloat16)
            parts_ref[0, start + k, :size] = high
            parts_ref[0, start + k, size:] = (value - high.astype(jnp.float32)).astype(jnp.bfloat16)

    @pl.when(place_ref[0] == 0)
    def _():
        split(own_ref, 0)
        split(other_ref, picks)

    @pl.when(place_ref[0] != 0)
    def _():
        split(other_ref, 0)
        split(own_ref, picks)


def split_operator(values, other, place):
    _, picks, size, depth = values.shape
    rows = other.shape[0]
    spec = pltpu.PrefetchScalarGridSpec(
        num_scalar_prefetch=1,
        grid=(rows,),
        in_specs=[
            pl.BlockSpec((1, picks, size, depth), lambda i, place_ref: (place_ref[0] * rows + i, 0, 0, 0)),
            pl.BlockSpec((1, picks, size, depth), lambda i, place_ref: (i, 0, 0, 0)),
        ],
        out_specs=pl.BlockSpec((1, 2 * picks, 2 * size, depth), lambda i, place_ref: (i, 0, 0, 0)),
    )
    return pl.pallas_call(
        split_kernel,
        grid_spec=spec,
        out_shape=jax.ShapeDtypeStruct((rows, 2 * picks, 2 * size, depth), jnp.bfloat16),
        compiler_params=pltpu.CompilerParams(vmem_limit_bytes=44 * 2**20),
        name="split_operator",
    )(place, values, other)


def apply_kernel(index_ref, parts_ref, gathered_ref, *refs):
    result_ref, tiles = refs[-2:]
    step = pl.program_id(0)
    rows, picks, _, size = parts_ref.shape
    pieces, groups, span, piece_rows = gathered_ref.shape
    per_piece = piece_rows // size

    @pl.when(step == 0)
    def _():
        for group in range(groups):
            for piece in range(pieces):
                for j in range(per_piece):
                    tile = gathered_ref[piece, group, :, j * size : (j + 1) * size]
                    high = tile.astype(jnp.bfloat16).astype(jnp.float32)
                    both = jnp.concatenate([high, tile - high], axis=0)
                    tiles[(group * pieces + piece) * per_piece + j] = both.T.astype(jnp.bfloat16)

    found = []
    for i in range(rows):
        base = (step * rows + i) * picks
        picked = jnp.concatenate([tiles[index_ref[base + k]] for k in range(picks)], axis=0)
        block = jnp.concatenate([parts_ref[i, k] for k in range(picks)], axis=1)
        product = jnp.dot(block, picked, preferred_element_type=jnp.float32)
        both = (product[:size] + product[size:]).T
        found.append(both[:span] + both[span:])
    result_ref[...] = jnp.concatenate(found, axis=1)


def apply_operator(parts, index, gathered, *after):
    block_rows, picks, twice, size = parts.shape
    pieces, groups, span, piece_rows = gathered.shape
    rows = divisor_up_to(block_rows, 2)
    spec = pltpu.PrefetchScalarGridSpec(
        num_scalar_prefetch=1,
        grid=(block_rows // rows,),
        in_specs=[
            pl.BlockSpec((rows, picks, twice, size), lambda step, *_: (step, 0, 0, 0)),
            pl.BlockSpec((pieces, groups, span, piece_rows), lambda step, *_: (0, 0, 0, 0)),
        ]
        + [pl.BlockSpec(memory_space=pl.ANY)] * len(after),
        out_specs=pl.BlockSpec((span, rows * size), lambda step, *_: (0, step)),
        scratch_shapes=[pltpu.VMEM((groups * pieces * piece_rows // size, size, 2 * span), jnp.bfloat16)],
    )
    return pl.pallas_call(
        apply_kernel,
        grid_spec=spec,
        out_shape=jax.ShapeDtypeStruct((span, block_rows * size), jnp.float32),
        compiler_params=pltpu.CompilerParams(vmem_limit_bytes=44 * 2**20),
        cost_estimate=pl.CostEstimate(flops=0, bytes_accessed=gathered.size, transcendentals=0),
        name="apply_operator",
    )(index, parts, gathered, *after)


def sum_kernel(which_ref, arrived_ref, store_ref, *refs):
    refs[-1][...] = arrived_ref[...] + store_ref[0]


def sum_with(arrived, store, which, *after):
    spec = pltpu.PrefetchScalarGridSpec(
        num_scalar_prefetch=1,
        grid=(1,),
        in_specs=[
            pl.BlockSpec(arrived.shape, lambda i, which_ref: (0, 0)),
            pl.BlockSpec((1,) + arrived.shape, lambda i, which_ref: (which_ref[0], 0, 0)),
        ]
        + [pl.BlockSpec(memory_space=pl.ANY)] * len(after),
        out_specs=pl.BlockSpec(arrived.shape, lambda i, which_ref: (0, 0)),
    )
    return pl.pallas_call(
        sum_kernel,
        grid_spec=spec,
        out_shape=jax.ShapeDtypeStruct(arrived.shape, arrived.dtype),
        compiler_params=pltpu.CompilerParams(vmem_limit_bytes=44 * 2**20),
        name="sum_with",
    )(which.reshape(1), arrived, store, *after)


def shards(sources, tr_vals, tr_cols, rf_vals, rf_cols):
    source = sources[0, 0, 0]
    piece_rows, columns = source.shape
    batches, delay = BATCHES, DELAY
    span = columns // batches
    length = lax.axis_size("slab")
    position = lax.axis_index("slab")
    place = lax.axis_index("row")
    source = source.T.reshape(batches, span, piece_rows)
    group_blocks = lax.axis_size("col") * piece_rows // tr_vals.shape[-1]

    def halves(values, columns):
        half = values.shape[0] // 2
        swap = [(0, 1), (1, 0)]

        def other_half(array):
            return lax.ppermute(lax.dynamic_slice_in_dim(array, (1 - place) * half, half, 0), "row", swap)

        own = lax.dynamic_slice_in_dim(columns, place * half, half, 0)
        other = other_half(columns)
        first = jnp.where(place == 0, own, other)
        second = jnp.where(place == 0, other, own) + group_blocks
        index = jnp.concatenate([first, second], axis=1).reshape(-1)
        return split_operator(values, other_half(values), place.reshape(1)), index

    trans = halves(tr_vals[0, 0, 0], tr_cols[0, 0, 0])
    refl = halves(rf_vals[0, 0, 0], rf_cols[0, 0, 0])

    def gather(piece):
        return lax.all_gather(piece, ("col", "row"), axis=0).reshape((-1, 2) + piece.shape)

    moments = batches + delay * (length - 1)

    def sweep(first, start, steps, reflect):
        def incident_of(moment):
            offset = position if steps > 0 else length - 1 - position
            which = jnp.clip(moment - delay * offset, 0, batches - 1) + start
            if moment < delay:
                return lax.dynamic_index_in_dim(first, which, 0, keepdims=False)
            arrived = passed_along(moved[moment - delay], "slab", steps)
            return sum_with(arrived, first, which, *reflected[moment - delay : moment - delay + 1])

        moved, reflected = [], []
        incident = incident_of(0)
        gathered = gather(incident)
        for moment in range(moments):
            if moment + 1 < moments:
                incident = incident_of(moment + 1)
                coming = gather(incident)
            moved.append(apply_operator(*trans, gathered, incident, *reflected[-1:]))
            if reflect:
                reflected.append(apply_operator(*refl, gathered, moved[-1]))
            gathered = coming
        return jnp.stack(moved), jnp.stack(reflected) if reflect else None

    downs, reflected = sweep(source, 0, 1, True)
    ups, _ = sweep(reflected, delay * position, -1, False)
    down = lax.dynamic_slice_in_dim(downs, delay * position, batches, 0)
    up = lax.dynamic_slice_in_dim(ups, delay * (length - 1 - position), batches, 0)
    total = (down + up).reshape(columns, piece_rows).T
    return total[None, None, None]


def solution(mesh):
    placed = (
        P("slab", "col", "row", None, None),
        P("slab", "col", "row", None, None, None, None),
        P("slab", "col", "row", None, None),
        P("slab", "col", "row", None, None, None, None),
        P("slab", "col", "row", None, None),
    )
    return jax.shard_map(
        shards,
        mesh=mesh,
        in_specs=placed,
        out_specs=P("slab", "col", "row", None, None),
        check_vma=False,
    )
```

```python
import jax
import jax.numpy as jnp
from jax import lax
from jax.experimental import pallas as pl
from jax.experimental.pallas import tpu as pltpu
from jax.sharding import PartitionSpec as P

LANES = 128
DELAY = 2
SLOTS = 4
VMEM_BYTES = 44 * 2**20
TOKEN = jax.ShapeDtypeStruct((8, LANES), jnp.float32)
TOKEN_SPEC = pl.BlockSpec(TOKEN.shape, lambda *_: (0, 0))


def passed_along(value, axis, steps):
    count = lax.axis_size(axis)
    initial, last = (max(0, -steps), min(count, count - steps))
    return lax.ppermute(value, axis, [(source, source + steps) for source in range(initial, last)])


def pack_kernel(rows_ref, packed_ref):
    batches, _, size, lanes = packed_ref.shape
    pack = rows_ref.shape[0] // size
    span = lanes // pack
    for batch in range(batches):
        found = [rows_ref[q * size : (q + 1) * size, batch * span : (batch + 1) * span] for q in range(pack)]
        packed_ref[batch, 0] = jnp.concatenate(found, axis=1)


def unpack_kernel(packed_ref, rows_ref):
    batches, _, size, lanes = packed_ref.shape
    pack = rows_ref.shape[0] // size
    span = lanes // pack
    for q in range(pack):
        found = [packed_ref[batch, 0, :, q * span : (q + 1) * span] for batch in range(batches)]
        rows_ref[q * size : (q + 1) * size, :] = jnp.concatenate(found, axis=1)


def packed_trace(rows, batches, pack, size):
    groups = rows.shape[0] // (pack * size)
    return pl.pallas_call(
        pack_kernel,
        grid=(groups,),
        in_specs=[pl.BlockSpec((pack * size, rows.shape[1]), lambda i: (i, 0))],
        out_specs=pl.BlockSpec((batches, 1, size, LANES), lambda i: (0, i, 0, 0)),
        out_shape=jax.ShapeDtypeStruct((batches, groups, size, LANES), rows.dtype),
        compiler_params=pltpu.CompilerParams(vmem_limit_bytes=VMEM_BYTES),
        name="pack_trace",
    )(rows)


def unpacked_trace(packed, pack):
    batches, groups, size, lanes = packed.shape
    columns = batches * (lanes // pack)
    return pl.pallas_call(
        unpack_kernel,
        grid=(groups,),
        in_specs=[pl.BlockSpec((batches, 1, size, lanes), lambda i: (0, i, 0, 0))],
        out_specs=pl.BlockSpec((pack * size, columns), lambda i: (i, 0)),
        out_shape=jax.ShapeDtypeStruct((groups * pack * size, columns), packed.dtype),
        compiler_params=pltpu.CompilerParams(vmem_limit_bytes=VMEM_BYTES),
        name="unpack_trace",
    )(packed)


def split_kernel(place_ref, own_ref, other_ref, parts_ref):
    picks, size = own_ref.shape[1:3]
    for start, values_ref in ((0, own_ref), (picks, other_ref)):
        for k in range(picks):
            value = values_ref[0, k]
            high = value.astype(jnp.bfloat16)
            parts_ref[0, start + k, :size] = high
            parts_ref[0, start + k, size:] = (value - high.astype(jnp.float32)).astype(jnp.bfloat16)


def split_operator(values, other, place):
    _, picks, size, depth = values.shape
    rows = other.shape[0]
    spec = pltpu.PrefetchScalarGridSpec(
        num_scalar_prefetch=1,
        grid=(rows,),
        in_specs=[
            pl.BlockSpec((1, picks, size, depth), lambda i, place_ref: (place_ref[0] * rows + i, 0, 0, 0)),
            pl.BlockSpec((1, picks, size, depth), lambda i, place_ref: (i, 0, 0, 0)),
        ],
        out_specs=pl.BlockSpec((1, 2 * picks, 2 * size, depth), lambda i, place_ref: (i, 0, 0, 0)),
    )
    return pl.pallas_call(
        split_kernel,
        grid_spec=spec,
        out_shape=jax.ShapeDtypeStruct((rows, 2 * picks, 2 * size, depth), jnp.bfloat16),
        compiler_params=pltpu.CompilerParams(vmem_limit_bytes=VMEM_BYTES),
        name="split_operator",
    )(place, values, other)


def apply_kernel(pack, index_ref, parts_ref, own_ref, other_ref, *refs):
    result_ref, token_ref, slots, tiles, arrived = refs[-5:]
    row, rows = pl.program_id(0), pl.num_programs(0)
    count, picks, twice, _ = slots.shape
    size = twice // 2
    pieces, groups, _, lanes = own_ref.shape
    span = lanes // pack

    def fetch(which):
        slot = lax.rem(which, count)
        return pltpu.make_async_copy(parts_ref.at[which], slots.at[slot], arrived.at[slot])

    @pl.when(row == 0)
    def _():
        for ahead in range(min(count - 1, parts_ref.shape[0])):
            fetch(ahead).start()

    @pl.when(row + count - 1 < rows)
    def _():
        fetch(row + count - 1).start()

    @pl.when(row == 0)
    def _():
        token_ref[...] = jnp.zeros_like(token_ref)
        lane = lax.broadcasted_iota(jnp.int32, (size, 2 * lanes), 1) % lanes // span
        masks = [(lane == q).astype(jnp.float32).astype(jnp.bfloat16) for q in range(pack)]
        for start, ref in ((0, own_ref), (pieces * groups, other_ref)):
            for piece in range(pieces):
                for group in range(groups):
                    tile = ref[piece, group]
                    high = tile.astype(jnp.bfloat16)
                    low = (tile - high.astype(jnp.float32)).astype(jnp.bfloat16)
                    both = jnp.concatenate([high, low], axis=1)
                    base = (start + piece * groups + group) * pack
                    for q in range(pack):
                        tiles[base + q] = both * masks[q] if pack > 1 else both

    fetch(row).wait()
    slot = lax.rem(row, count)
    picked = jnp.concatenate([tiles[index_ref[row * picks + k]] for k in range(picks)], axis=0)
    block = jnp.concatenate([slots[slot, k] for k in range(picks)], axis=1)
    product = jnp.dot(block, picked, preferred_element_type=jnp.float32)
    total = product[:size] + product[size:]
    total = total[:, :lanes] + total[:, lanes:]
    shift = span
    while shift < lanes:
        total = total + pltpu.roll(total, shift, 1)
        shift *= 2
    if pack == 1:
        result_ref[0] = total
    else:
        lane = lax.broadcasted_iota(jnp.int32, total.shape, 1)
        result_ref[0] = jnp.where(lane < lax.rem(row, pack) * span, result_ref[0], total)


def apply_operator(parts, index, pack, own, other, *after):
    rows, picks, twice, depth = parts.shape
    pieces, groups, size, lanes = own.shape
    whole = pl.BlockSpec(own.shape, lambda row, *_: (0, 0, 0, 0))
    spec = pltpu.PrefetchScalarGridSpec(
        num_scalar_prefetch=1,
        grid=(rows,),
        in_specs=[pl.BlockSpec(memory_space=pl.ANY), whole, whole]
        + [pl.BlockSpec(memory_space=pl.ANY)] * len(after),
        out_specs=[pl.BlockSpec((1, size, lanes), lambda row, *_: (row // pack, 0, 0)), TOKEN_SPEC],
        scratch_shapes=[
            pltpu.VMEM((SLOTS, picks, twice, depth), jnp.bfloat16),
            pltpu.VMEM((2 * pieces * groups * pack, size, 2 * lanes), jnp.bfloat16),
            pltpu.SemaphoreType.DMA((SLOTS,)),
        ],
    )

    def kernel(*refs):
        apply_kernel(pack, *refs)

    return pl.pallas_call(
        kernel,
        grid_spec=spec,
        out_shape=[jax.ShapeDtypeStruct((groups, size, lanes), jnp.float32), TOKEN],
        compiler_params=pltpu.CompilerParams(vmem_limit_bytes=VMEM_BYTES),
        cost_estimate=pl.CostEstimate(flops=0, bytes_accessed=own.size, transcendentals=0),
        name="apply_operator",
    )(index, parts, own, other, *after)


def sum_kernel(which_ref, arrived_ref, store_ref, *refs):
    copies_ref, token_ref = refs[-2:]
    total = arrived_ref[...] + store_ref[0]
    for copy in range(copies_ref.shape[0]):
        copies_ref[copy] = total
    token_ref[...] = jnp.zeros_like(token_ref)


def sum_with(copies, arrived, store, which, *after):
    spec = pltpu.PrefetchScalarGridSpec(
        num_scalar_prefetch=1,
        grid=(1,),
        in_specs=[
            pl.BlockSpec(arrived.shape, lambda i, which_ref: (0, 0, 0)),
            pl.BlockSpec((1,) + arrived.shape, lambda i, which_ref: (which_ref[0], 0, 0, 0)),
        ]
        + [pl.BlockSpec(memory_space=pl.ANY)] * len(after),
        out_specs=[
            pl.BlockSpec((copies,) + arrived.shape, lambda i, which_ref: (0, 0, 0, 0)),
            TOKEN_SPEC,
        ],
    )
    return pl.pallas_call(
        sum_kernel,
        grid_spec=spec,
        out_shape=[jax.ShapeDtypeStruct((copies,) + arrived.shape, arrived.dtype), TOKEN],
        compiler_params=pltpu.CompilerParams(vmem_limit_bytes=VMEM_BYTES),
        name="sum_with",
    )(which.reshape(1), arrived, store, *after)


def shards(sources, tr_vals, tr_cols, rf_vals, rf_cols):
    source = sources[0, 0, 0]
    piece_rows, columns = source.shape
    size = tr_vals.shape[-1]
    blocks = piece_rows // size
    pack = next(n for n in (4, 2, 1) if blocks % n == 0)
    batches, delay = columns // (LANES // pack), DELAY
    length, pieces = lax.axis_size("slab"), lax.axis_size("col")
    position = lax.axis_index("slab")
    place = lax.axis_index("row")
    swap = [(0, 1), (1, 0)]
    source = packed_trace(source, batches, pack, size)

    def halves(values, columns):
        half = values.shape[0] // 2

        def other_half(array):
            return lax.ppermute(lax.dynamic_slice_in_dim(array, (1 - place) * half, half, 0), "row", swap)

        own = lax.dynamic_slice_in_dim(columns, place * half, half, 0)
        index = jnp.concatenate([own, other_half(columns) + pieces * blocks], axis=1).reshape(-1)
        return split_operator(values, other_half(values), place.reshape(1)), index, pack

    trans = halves(tr_vals[0, 0, 0], tr_cols[0, 0, 0])
    refl = halves(rf_vals[0, 0, 0], rf_cols[0, 0, 0])

    def gather(copies):
        gathered = lax.all_to_all(copies, "col", 0, 0)
        return gathered, lax.ppermute(gathered, "row", swap)

    moments = batches + delay * (length - 1)

    def sweep(first, start, steps, reflect):
        def incident_of(moment):
            offset = position if steps > 0 else length - 1 - position
            which = jnp.clip(moment - delay * offset, 0, batches - 1) + start
            if moment < delay:
                piece = lax.dynamic_index_in_dim(first, which, 0, keepdims=False)
                return jnp.broadcast_to(piece[None], (pieces,) + piece.shape), None
            arrived = passed_along(moved[moment - delay], "slab", steps)
            return sum_with(pieces, arrived, first, which, *tokens[moment - delay : moment - delay + 1])

        moved, reflected, tokens = [], [], []
        incident, _ = incident_of(0)
        gathered = gather(incident)
        for moment in range(moments):
            after = tokens[-1:]
            if moment + 1 < moments:
                incident, token = incident_of(moment + 1)
                coming = gather(incident)
                after = after + ([] if token is None else [token])
            product, token = apply_operator(*trans, *gathered, *after)
            moved.append(product)
            if reflect:
                product, token = apply_operator(*refl, *gathered, token)
                reflected.append(product)
                tokens.append(token)
            gathered = coming
        return jnp.stack(moved), jnp.stack(reflected) if reflect else None

    downs, reflected = sweep(source, 0, 1, True)
    ups, _ = sweep(reflected, delay * position, -1, False)
    down = lax.dynamic_slice_in_dim(downs, delay * position, batches, 0)
    up = lax.dynamic_slice_in_dim(ups, delay * (length - 1 - position), batches, 0)
    return unpacked_trace(down + up, pack)[None, None, None]


def solution(mesh):
    placed = (
        P("slab", "col", "row", None, None),
        P("slab", "col", "row", None, None, None, None),
        P("slab", "col", "row", None, None),
        P("slab", "col", "row", None, None, None, None),
        P("slab", "col", "row", None, None),
    )
    return jax.shard_map(
        shards,
        mesh=mesh,
        in_specs=placed,
        out_specs=P("slab", "col", "row", None, None),
        check_vma=False,
    )
```

```python
import jax
import jax.numpy as jnp
from jax import lax
from jax.experimental import pallas as pl
from jax.experimental.pallas import tpu as pltpu
from jax.sharding import PartitionSpec as P

LANES = 128
DELAY = 2
SLOTS = 8
VMEM_BYTES = 44 * 2**20
TOKEN = jax.ShapeDtypeStruct((8, LANES), jnp.float32)
TOKEN_SPEC = pl.BlockSpec(TOKEN.shape, lambda *_: (0, 0))


def passed_along(value, axis, steps):
    count = lax.axis_size(axis)
    initial, last = (max(0, -steps), min(count, count - steps))
    return lax.ppermute(value, axis, [(source, source + steps) for source in range(initial, last)])


def pack_kernel(rows_ref, packed_ref):
    batches, _, size, lanes = packed_ref.shape
    pack = rows_ref.shape[0] // size
    span = lanes // pack
    for batch in range(batches):
        found = [rows_ref[q * size : (q + 1) * size, batch * span : (batch + 1) * span] for q in range(pack)]
        packed_ref[batch, 0] = jnp.concatenate(found, axis=1)


def unpack_kernel(packed_ref, rows_ref):
    batches, _, size, lanes = packed_ref.shape
    pack = rows_ref.shape[0] // size
    span = lanes // pack
    for q in range(pack):
        found = [packed_ref[batch, 0, :, q * span : (q + 1) * span] for batch in range(batches)]
        rows_ref[q * size : (q + 1) * size, :] = jnp.concatenate(found, axis=1)


def packed_trace(rows, batches, pack, size):
    groups = rows.shape[0] // (pack * size)
    return pl.pallas_call(
        pack_kernel,
        grid=(groups,),
        in_specs=[pl.BlockSpec((pack * size, rows.shape[1]), lambda i: (i, 0))],
        out_specs=pl.BlockSpec((batches, 1, size, LANES), lambda i: (0, i, 0, 0)),
        out_shape=jax.ShapeDtypeStruct((batches, groups, size, LANES), rows.dtype),
        compiler_params=pltpu.CompilerParams(vmem_limit_bytes=VMEM_BYTES),
        name="pack_trace",
    )(rows)


def unpacked_trace(packed, pack):
    batches, groups, size, lanes = packed.shape
    columns = batches * (lanes // pack)
    return pl.pallas_call(
        unpack_kernel,
        grid=(groups,),
        in_specs=[pl.BlockSpec((batches, 1, size, lanes), lambda i: (0, i, 0, 0))],
        out_specs=pl.BlockSpec((pack * size, columns), lambda i: (i, 0)),
        out_shape=jax.ShapeDtypeStruct((groups * pack * size, columns), packed.dtype),
        compiler_params=pltpu.CompilerParams(vmem_limit_bytes=VMEM_BYTES),
        name="unpack_trace",
    )(packed)


def split_kernel(place_ref, own_ref, other_ref, parts_ref):
    picks, size = own_ref.shape[1:3]
    for start, values_ref in ((0, own_ref), (picks, other_ref)):
        for k in range(picks):
            value = values_ref[0, k]
            high = value.astype(jnp.bfloat16)
            parts_ref[0, start + k, :size] = high
            parts_ref[0, start + k, size:] = (value - high.astype(jnp.float32)).astype(jnp.bfloat16)


def split_operator(values, other, place):
    _, picks, size, depth = values.shape
    rows = other.shape[0]
    spec = pltpu.PrefetchScalarGridSpec(
        num_scalar_prefetch=1,
        grid=(rows,),
        in_specs=[
            pl.BlockSpec((1, picks, size, depth), lambda i, place_ref: (place_ref[0] * rows + i, 0, 0, 0)),
            pl.BlockSpec((1, picks, size, depth), lambda i, place_ref: (i, 0, 0, 0)),
        ],
        out_specs=pl.BlockSpec((1, 2 * picks, 2 * size, depth), lambda i, place_ref: (i, 0, 0, 0)),
    )
    return pl.pallas_call(
        split_kernel,
        grid_spec=spec,
        out_shape=jax.ShapeDtypeStruct((rows, 2 * picks, 2 * size, depth), jnp.bfloat16),
        compiler_params=pltpu.CompilerParams(vmem_limit_bytes=VMEM_BYTES),
        name="split_operator",
    )(place, values, other)


def apply_kernel(pack, index_ref, parts_ref, own_ref, other_ref, *refs):
    result_ref, token_ref, slots, tiles, arrived = refs[-5:]
    row, rows = pl.program_id(0), pl.num_programs(0)
    count, picks, twice, _ = slots.shape
    size = twice // 2
    pieces, groups, _, lanes = own_ref.shape
    span = lanes // pack

    def fetch(which):
        slot = lax.rem(which, count)
        return pltpu.make_async_copy(parts_ref.at[which], slots.at[slot], arrived.at[slot])

    @pl.when(row == 0)
    def _():
        for ahead in range(min(count - 1, parts_ref.shape[0])):
            fetch(ahead).start()

    @pl.when(row + count - 1 < rows)
    def _():
        fetch(row + count - 1).start()

    @pl.when(row == 0)
    def _():
        token_ref[...] = jnp.zeros_like(token_ref)
        left = lax.broadcasted_iota(jnp.int32, (size, lanes), 1) < span
        for start, ref in ((0, own_ref), (pieces * groups, other_ref)):
            for piece in range(pieces):
                for group in range(groups):
                    tile = ref[piece, group]
                    high = tile.astype(jnp.bfloat16).astype(jnp.float32)
                    low = tile - high
                    base = (start + piece * groups + group) * pack
                    if pack == 1:
                        tiles[base] = jnp.concatenate([high, low], axis=1).astype(jnp.bfloat16)
                    else:
                        first = jnp.where(left, high, pltpu.roll(low, span, 1))
                        second = jnp.where(left, pltpu.roll(high, span, 1), low)
                        tiles[base] = first.astype(jnp.bfloat16)
                        tiles[base + 1] = second.astype(jnp.bfloat16)

    fetch(row).wait()
    slot = lax.rem(row, count)
    picked = jnp.concatenate([tiles[index_ref[row * picks + k]] for k in range(picks)], axis=0)
    block = jnp.concatenate([slots[slot, k] for k in range(picks)], axis=1)
    product = jnp.dot(block, picked, preferred_element_type=jnp.float32)
    total = product[:size] + product[size:]
    if pack == 1:
        result_ref[0] = total[:, :lanes] + total[:, lanes:]
    else:
        total = total + pltpu.roll(total, span, 1)
        lane = lax.broadcasted_iota(jnp.int32, total.shape, 1)
        result_ref[0] = jnp.where(lane < lax.rem(row, pack) * span, result_ref[0], total)


def apply_operator(parts, index, pack, own, other, *after):
    rows, picks, twice, depth = parts.shape
    pieces, groups, size, lanes = own.shape
    whole = pl.BlockSpec(own.shape, lambda row, *_: (0, 0, 0, 0))
    spec = pltpu.PrefetchScalarGridSpec(
        num_scalar_prefetch=1,
        grid=(rows,),
        in_specs=[pl.BlockSpec(memory_space=pl.ANY), whole, whole]
        + [pl.BlockSpec(memory_space=pl.ANY)] * len(after),
        out_specs=[pl.BlockSpec((1, size, lanes), lambda row, *_: (row // pack, 0, 0)), TOKEN_SPEC],
        scratch_shapes=[
            pltpu.VMEM((SLOTS, picks, twice, depth), jnp.bfloat16),
            pltpu.VMEM((2 * pieces * groups * pack, size, 2 * lanes // pack), jnp.bfloat16),
            pltpu.SemaphoreType.DMA((SLOTS,)),
        ],
    )

    def kernel(*refs):
        apply_kernel(pack, *refs)

    return pl.pallas_call(
        kernel,
        grid_spec=spec,
        out_shape=[jax.ShapeDtypeStruct((groups, size, lanes), jnp.float32), TOKEN],
        compiler_params=pltpu.CompilerParams(vmem_limit_bytes=VMEM_BYTES),
        cost_estimate=pl.CostEstimate(flops=0, bytes_accessed=own.size, transcendentals=0),
        name="apply_operator",
    )(index, parts, own, other, *after)


def sum_kernel(which_ref, arrived_ref, store_ref, *refs):
    total_ref, token_ref = refs[-2:]
    total_ref[...] = arrived_ref[...] + store_ref[0]
    token_ref[...] = jnp.zeros_like(token_ref)


def sum_with(arrived, store, which, *after):
    spec = pltpu.PrefetchScalarGridSpec(
        num_scalar_prefetch=1,
        grid=(1,),
        in_specs=[
            pl.BlockSpec(arrived.shape, lambda i, which_ref: (0, 0, 0)),
            pl.BlockSpec((1,) + arrived.shape, lambda i, which_ref: (which_ref[0], 0, 0, 0)),
        ]
        + [pl.BlockSpec(memory_space=pl.ANY)] * len(after),
        out_specs=[
            pl.BlockSpec(arrived.shape, lambda i, which_ref: (0, 0, 0)),
            TOKEN_SPEC,
        ],
    )
    return pl.pallas_call(
        sum_kernel,
        grid_spec=spec,
        out_shape=[jax.ShapeDtypeStruct(arrived.shape, arrived.dtype), TOKEN],
        compiler_params=pltpu.CompilerParams(vmem_limit_bytes=VMEM_BYTES),
        name="sum_with",
    )(which.reshape(1), arrived, store, *after)


def shards(sources, tr_vals, tr_cols, rf_vals, rf_cols):
    source = sources[0, 0, 0]
    piece_rows, columns = source.shape
    size = tr_vals.shape[-1]
    blocks = piece_rows // size
    pack = 2 if blocks % 2 == 0 else 1
    batches, delay = columns // (LANES // pack), DELAY
    length, pieces = lax.axis_size("slab"), lax.axis_size("col")
    position = lax.axis_index("slab")
    place = lax.axis_index("row")
    swap = [(0, 1), (1, 0)]
    source = packed_trace(source, batches, pack, size)

    def halves(values, columns):
        half = values.shape[0] // 2

        def other_half(array):
            return lax.ppermute(lax.dynamic_slice_in_dim(array, (1 - place) * half, half, 0), "row", swap)

        own = lax.dynamic_slice_in_dim(columns, place * half, half, 0)
        index = jnp.concatenate([own, other_half(columns) + pieces * blocks], axis=1).reshape(-1)
        return split_operator(values, other_half(values), place.reshape(1)), index, pack

    trans = halves(tr_vals[0, 0, 0], tr_cols[0, 0, 0])
    refl = halves(rf_vals[0, 0, 0], rf_cols[0, 0, 0])

    def gather(piece):
        gathered = lax.all_gather(piece, "col", axis=0)
        return gathered, lax.ppermute(gathered, "row", swap)

    moments = batches + delay * (length - 1)

    def sweep(first, start, steps, reflect):
        def incident_of(moment):
            offset = position if steps > 0 else length - 1 - position
            which = jnp.clip(moment - delay * offset, 0, batches - 1) + start
            if moment < delay:
                return lax.dynamic_index_in_dim(first, which, 0, keepdims=False), None
            arrived = passed_along(moved[moment - delay], "slab", steps)
            return sum_with(arrived, first, which, *tokens[moment - delay : moment - delay + 1])

        moved, reflected, tokens = [], [], []
        incident, _ = incident_of(0)
        gathered = gather(incident)
        for moment in range(moments):
            after = tokens[-1:]
            if moment + 1 < moments:
                incident, token = incident_of(moment + 1)
                coming = gather(incident)
                after = after + ([] if token is None else [token])
            product, token = apply_operator(*trans, *gathered, *after)
            moved.append(product)
            if reflect:
                product, token = apply_operator(*refl, *gathered, token)
                reflected.append(product)
                tokens.append(token)
            gathered = coming
        return jnp.stack(moved), jnp.stack(reflected) if reflect else None

    downs, reflected = sweep(source, 0, 1, True)
    ups, _ = sweep(reflected, delay * position, -1, False)
    down = lax.dynamic_slice_in_dim(downs, delay * position, batches, 0)
    up = lax.dynamic_slice_in_dim(ups, delay * (length - 1 - position), batches, 0)
    return unpacked_trace(down + up, pack)[None, None, None]


def solution(mesh):
    placed = (
        P("slab", "col", "row", None, None),
        P("slab", "col", "row", None, None, None, None),
        P("slab", "col", "row", None, None),
        P("slab", "col", "row", None, None, None, None),
        P("slab", "col", "row", None, None),
    )
    return jax.shard_map(
        shards,
        mesh=mesh,
        in_specs=placed,
        out_specs=P("slab", "col", "row", None, None),
        check_vma=False,
    )
```

```python
import jax
import jax.numpy as jnp
from jax import lax
from jax.experimental import pallas as pl
from jax.experimental.pallas import tpu as pltpu
from jax.sharding import PartitionSpec as P

LANES = 128
DELAY = 2
SLOTS = 8
FRACTION = 3
VMEM_BYTES = 44 * 2**20
TOKEN = jax.ShapeDtypeStruct((8, LANES), jnp.float32)
TOKEN_SPEC = pl.BlockSpec(TOKEN.shape, lambda *_: (0, 0))


def divisor_up_to(number, limit):
    return max(n for n in range(1, limit + 1) if number % n == 0)


def passed_along(value, axis, steps):
    count = lax.axis_size(axis)
    initial, last = (max(0, -steps), min(count, count - steps))
    return lax.ppermute(value, axis, [(source, source + steps) for source in range(initial, last)])


def pack_kernel(rows_ref, packed_ref):
    batches, _, size, lanes = packed_ref.shape
    pack = rows_ref.shape[0] // size
    span = lanes // pack
    for batch in range(batches):
        found = [rows_ref[q * size : (q + 1) * size, batch * span : (batch + 1) * span] for q in range(pack)]
        packed_ref[batch, 0] = jnp.concatenate(found, axis=1)


def unpack_kernel(*refs):
    rows_ref = refs[-1]
    _, size, lanes = refs[0].shape
    pack = rows_ref.shape[0] // size
    span = lanes // pack
    for q in range(pack):
        found = [ref[0, :, q * span : (q + 1) * span] for ref in refs[:-1]]
        rows_ref[q * size : (q + 1) * size, :] = jnp.concatenate(found, axis=1)


def packed_trace(rows, batches, pack, size):
    groups = rows.shape[0] // (pack * size)
    return pl.pallas_call(
        pack_kernel,
        grid=(groups,),
        in_specs=[pl.BlockSpec((pack * size, rows.shape[1]), lambda i: (i, 0))],
        out_specs=pl.BlockSpec((batches, 1, size, LANES), lambda i: (0, i, 0, 0)),
        out_shape=jax.ShapeDtypeStruct((batches, groups, size, LANES), rows.dtype),
        compiler_params=pltpu.CompilerParams(vmem_limit_bytes=VMEM_BYTES),
        name="pack_trace",
    )(rows)


def unpacked_trace(packed, pack):
    groups, size, lanes = packed[0].shape
    columns = len(packed) * (lanes // pack)
    return pl.pallas_call(
        unpack_kernel,
        grid=(groups,),
        in_specs=[pl.BlockSpec((1, size, lanes), lambda i: (i, 0, 0))] * len(packed),
        out_specs=pl.BlockSpec((pack * size, columns), lambda i: (i, 0)),
        out_shape=jax.ShapeDtypeStruct((groups * pack * size, columns), jnp.float32),
        compiler_params=pltpu.CompilerParams(vmem_limit_bytes=VMEM_BYTES),
        name="unpack_trace",
    )(*packed)


def in_hbm(array):
    return pltpu.with_memory_space_constraint(array, pltpu.HBM)


def half_kernel(place_ref, values_ref, *refs):
    refs[-1][...] = values_ref[...]


def other_half(values, place, after):
    rows = values.shape[0] // 2
    step = divisor_up_to(rows, 3)
    block = (step,) + values.shape[1:]
    spec = pltpu.PrefetchScalarGridSpec(
        num_scalar_prefetch=1,
        grid=(rows // step,),
        in_specs=[
            pl.BlockSpec(block, lambda i, place_ref: ((1 - place_ref[0]) * (rows // step) + i, 0, 0, 0)),
            pl.BlockSpec(memory_space=pl.ANY),
        ],
        out_specs=pl.BlockSpec(block, lambda i, place_ref: (i, 0, 0, 0)),
    )
    return pl.pallas_call(
        half_kernel,
        grid_spec=spec,
        out_shape=jax.ShapeDtypeStruct((rows,) + values.shape[1:], values.dtype),
        compiler_params=pltpu.CompilerParams(vmem_limit_bytes=VMEM_BYTES),
        name="other_half",
    )(place, values, after)


def split_kernel(place_ref, own_ref, other_ref, *refs):
    parts_ref = refs[-1]
    picks, size = own_ref.shape[1:3]
    for start, values_ref in ((0, own_ref), (picks, other_ref)):
        for k in range(picks):
            value = values_ref[0, k]
            high = value.astype(jnp.bfloat16)
            parts_ref[0, start + k, :size] = high
            parts_ref[0, start + k, size:] = (value - high.astype(jnp.float32)).astype(jnp.bfloat16)


def split_operator(values, other, place, after):
    _, picks, size, depth = values.shape
    rows = other.shape[0]
    spec = pltpu.PrefetchScalarGridSpec(
        num_scalar_prefetch=1,
        grid=(rows,),
        in_specs=[
            pl.BlockSpec((1, picks, size, depth), lambda i, place_ref: (place_ref[0] * rows + i, 0, 0, 0)),
            pl.BlockSpec((1, picks, size, depth), lambda i, place_ref: (i, 0, 0, 0)),
            pl.BlockSpec(memory_space=pltpu.HBM),
        ],
        out_specs=pl.BlockSpec((1, 2 * picks, 2 * size, depth), lambda i, place_ref: (i, 0, 0, 0)),
    )
    return pl.pallas_call(
        split_kernel,
        grid_spec=spec,
        out_shape=jax.ShapeDtypeStruct((rows, 2 * picks, 2 * size, depth), jnp.bfloat16),
        compiler_params=pltpu.CompilerParams(vmem_limit_bytes=VMEM_BYTES),
        name="split_operator",
    )(place, values, other, in_hbm(after))


def apply_kernel(pack, counts, index_ref, parts_ref, *refs):
    sources = refs[: 2 * len(counts)]
    result_ref, token_ref, slots, tiles, held, arrived, landed = refs[-7:]
    row, rows = pl.program_id(0), pl.num_programs(0)
    count, picks, twice, _ = slots.shape
    size = twice // 2
    _, pieces, groups, _, lanes = held.shape
    span = lanes // pack

    def fetch(which):
        slot = lax.rem(which, count)
        return pltpu.make_async_copy(parts_ref.at[which], slots.at[slot], arrived.at[slot])

    def bring(half, part):
        place = held.at[half, :, pl.ds(sum(counts[:part]), counts[part])]
        number = half * len(counts) + part
        return pltpu.make_async_copy(sources[number], place, landed.at[number])

    @pl.when(row == 0)
    def _():
        for half in range(2):
            for part in range(len(counts)):
                bring(half, part).start()
        for ahead in range(min(count - 1, parts_ref.shape[0])):
            fetch(ahead).start()

    @pl.when(row + count - 1 < rows)
    def _():
        fetch(row + count - 1).start()

    @pl.when(row == 0)
    def _():
        token_ref[...] = jnp.zeros_like(token_ref)
        left = lax.broadcasted_iota(jnp.int32, (size, lanes), 1) < span
        for half in range(2):
            for part in range(len(counts)):
                bring(half, part).wait()
            for piece in range(pieces):
                for group in range(groups):
                    tile = held[half, piece, group]
                    high = tile.astype(jnp.bfloat16).astype(jnp.float32)
                    low = tile - high
                    base = ((half * pieces + piece) * groups + group) * pack
                    if pack == 1:
                        tiles[base] = jnp.concatenate([high, low], axis=1).astype(jnp.bfloat16)
                    else:
                        first = jnp.where(left, high, pltpu.roll(low, span, 1))
                        second = jnp.where(left, pltpu.roll(high, span, 1), low)
                        tiles[base] = first.astype(jnp.bfloat16)
                        tiles[base + 1] = second.astype(jnp.bfloat16)

    fetch(row).wait()
    slot = lax.rem(row, count)
    picked = jnp.concatenate([tiles[index_ref[row * picks + k]] for k in range(picks)], axis=0)
    block = jnp.concatenate([slots[slot, k] for k in range(picks)], axis=1)
    product = jnp.dot(block, picked, preferred_element_type=jnp.float32)
    total = product[:size] + product[size:]
    if pack == 1:
        result_ref[0] = total[:, :lanes] + total[:, lanes:]
    else:
        total = total + pltpu.roll(total, span, 1)
        lane = lax.broadcasted_iota(jnp.int32, total.shape, 1)
        result_ref[0] = jnp.where(lane < lax.rem(row, pack) * span, result_ref[0], total)


def apply_operator(parts, index, pack, own, other, after):
    rows, picks, twice, depth = parts.shape
    pieces, _, size, lanes = own[0].shape
    counts = [part.shape[1] for part in own]
    groups = sum(counts)
    spec = pltpu.PrefetchScalarGridSpec(
        num_scalar_prefetch=1,
        grid=(rows,),
        in_specs=[pl.BlockSpec(memory_space=pltpu.HBM)] * (1 + 2 * len(own))
        + [pl.BlockSpec(memory_space=pl.ANY)] * len(after),
        out_specs=[pl.BlockSpec((1, size, lanes), lambda row, *_: (row // pack, 0, 0)), TOKEN_SPEC],
        scratch_shapes=[
            pltpu.VMEM((SLOTS, picks, twice, depth), jnp.bfloat16),
            pltpu.VMEM((2 * pieces * groups * pack, size, 2 * lanes // pack), jnp.bfloat16),
            pltpu.VMEM((2, pieces, groups, size, lanes), jnp.float32),
            pltpu.SemaphoreType.DMA((SLOTS,)),
            pltpu.SemaphoreType.DMA((2 * len(own),)),
        ],
    )

    def kernel(*refs):
        apply_kernel(pack, counts, *refs)

    return pl.pallas_call(
        kernel,
        grid_spec=spec,
        out_shape=[jax.ShapeDtypeStruct((groups, size, lanes), jnp.float32), TOKEN],
        compiler_params=pltpu.CompilerParams(vmem_limit_bytes=VMEM_BYTES),
        cost_estimate=pl.CostEstimate(flops=0, bytes_accessed=own[0].size, transcendentals=0),
        name="apply_operator",
    )(index, *map(in_hbm, (parts, *own, *other)), *after)


def sum_kernel(terms, *refs):
    first_ref, rest_ref, token_ref = refs[-3:]
    count = first_ref.shape[0]
    first_ref[...] = sum(ref[:count] for ref in refs[:terms])
    rest = sum(ref[count:] for ref in refs[:terms])
    for copy in range(rest_ref.shape[0]):
        rest_ref[copy] = rest
    token_ref[...] = jnp.zeros_like(token_ref)


def sum_of(terms, first, copies, after):
    groups, size, lanes = terms[0].shape
    shapes = [(first, size, lanes), (copies, groups - first, size, lanes)]

    def kernel(*refs):
        sum_kernel(len(terms), *refs)

    return pl.pallas_call(
        kernel,
        grid=(1,),
        in_specs=[pl.BlockSpec((groups, size, lanes), lambda i: (0, 0, 0))] * len(terms)
        + [pl.BlockSpec(memory_space=pl.ANY)] * len(after),
        out_specs=[
            pl.BlockSpec(shapes[0], lambda i: (0, 0, 0)),
            pl.BlockSpec(shapes[1], lambda i: (0, 0, 0, 0)),
            TOKEN_SPEC,
        ],
        out_shape=[jax.ShapeDtypeStruct(shape, jnp.float32) for shape in shapes] + [TOKEN],
        compiler_params=pltpu.CompilerParams(vmem_limit_bytes=VMEM_BYTES),
        name="sum_of",
    )(*terms, *after)


def shards(sources, tr_vals, tr_cols, rf_vals, rf_cols):
    source = sources[0, 0, 0]
    piece_rows, columns = source.shape
    size = tr_vals.shape[-1]
    blocks = piece_rows // size
    pack = 2 if blocks % 2 == 0 else 1
    batches, delay = columns // (LANES // pack), DELAY
    length, pieces = lax.axis_size("slab"), lax.axis_size("col")
    last = length - 1
    position = lax.axis_index("slab")
    place = lax.axis_index("row")
    swap = [(0, 1), (1, 0)]
    source = packed_trace(source, batches, pack, size)
    groups = source.shape[1]
    first = groups - groups // FRACTION

    def operator(values, columns, copy_after, split_after):
        half = values.shape[0] // 2
        own = lax.dynamic_slice_in_dim(columns, place * half, half, 0)
        other = lax.dynamic_slice_in_dim(columns, (1 - place) * half, half, 0)
        index = jnp.concatenate([own, lax.ppermute(other, "row", swap) + pieces * blocks], axis=1)
        traded = lax.ppermute(other_half(values, place.reshape(1), copy_after), "row", swap)
        return split_operator(values, traded, place.reshape(1), split_after), index.reshape(-1), pack

    def by_position(choices):
        known = [choice for choice in choices if choice is not None]
        chosen = known[-1]
        for slab, choice in enumerate(choices):
            if choice is not None and choice is not chosen:
                chosen = jnp.where(position == slab, choice, chosen)
        return chosen

    def held(results, batch_of, shift):
        return by_position(
            [
                results[batch_of(slab) + shift(slab)] if 0 <= batch_of(slab) < batches else None
                for slab in range(length)
            ]
        )

    def gather(part, copies):
        own = (lax.all_gather(part, "col", axis=0), lax.all_to_all(copies, "col", 0, 0))
        return own, tuple(lax.ppermute(array, "row", swap) for array in own)

    moments = batches + delay * last
    downs, refls, ups, tokens = [], [], [], []

    def incident_of(moment):
        after = tokens[moment - delay : moment - delay + 1]
        if moment < moments:
            which = jnp.clip(moment - delay * position, 0, batches - 1)
            terms = [lax.dynamic_index_in_dim(source, which, 0, keepdims=False)]
            if moment >= delay:
                terms.append(passed_along(downs[moment - delay], "slab", 1))
        else:
            at = moment - moments
            terms = [held(refls, lambda slab: at - delay * (last - slab), lambda slab: delay * slab)]
            if at >= delay:
                terms.append(passed_along(ups[at - delay], "slab", -1))
        return sum_of(terms, first, pieces, after)

    part, copies, _ = incident_of(0)
    gathered = [gather(part, copies)]
    trans = operator(tr_vals[0, 0, 0], tr_cols[0, 0, 0], part, gathered[0][0][0])
    lag = max(0, min(delay, batches - 2))
    copied_after = part
    for moment in range(2 * moments):
        after = tokens[-1:]
        if moment + 1 < 2 * moments:
            part, copies, token = incident_of(moment + 1)
            gathered.append(gather(part, copies))
            after = after + [token]
        if moment == 0:
            after = after + [in_hbm(gathered[1][0][0])]
        product, token = apply_operator(*trans, *gathered[moment], after)
        (downs if moment < moments else ups).append(product)
        if moment == max(0, lag - 1):
            refl = operator(rf_vals[0, 0, 0], rf_cols[0, 0, 0], copied_after, token)
        if lag <= moment < moments + lag:
            product, token = apply_operator(*refl, *gathered[moment - lag], [token])
            refls.append(product)
        tokens.append(token)
    totals = [
        held(downs, lambda slab: batch, lambda slab: delay * slab)
        + held(ups, lambda slab: batch, lambda slab: delay * (last - slab))
        for batch in range(batches)
    ]
    return unpacked_trace(totals, pack)[None, None, None]


def solution(mesh):
    placed = (
        P("slab", "col", "row", None, None),
        P("slab", "col", "row", None, None, None, None),
        P("slab", "col", "row", None, None),
        P("slab", "col", "row", None, None, None, None),
        P("slab", "col", "row", None, None),
    )
    return jax.shard_map(
        shards,
        mesh=mesh,
        in_specs=placed,
        out_specs=P("slab", "col", "row", None, None),
        check_vma=False,
    )
```

```python
import jax
import jax.numpy as jnp
from jax import lax
from jax.experimental import pallas as pl
from jax.experimental.pallas import tpu as pltpu
from jax.sharding import PartitionSpec as P

LANES = 128
DELAY = 2
SLOTS = 8
VMEM_BYTES = 44 * 2**20
TOKEN = jax.ShapeDtypeStruct((8, LANES), jnp.float32)
TOKEN_SPEC = pl.BlockSpec(TOKEN.shape, lambda *_: (0, 0))


def divisor_up_to(number, limit):
    return max(n for n in range(1, limit + 1) if number % n == 0)


def passed_along(value, axis, steps):
    count = lax.axis_size(axis)
    initial, last = (max(0, -steps), min(count, count - steps))
    return lax.ppermute(value, axis, [(source, source + steps) for source in range(initial, last)])


def pack_kernel(rows_ref, packed_ref):
    batches, _, size, lanes = packed_ref.shape
    pack = rows_ref.shape[0] // size
    span = lanes // pack
    for batch in range(batches):
        found = [rows_ref[q * size : (q + 1) * size, batch * span : (batch + 1) * span] for q in range(pack)]
        packed_ref[batch, 0] = jnp.concatenate(found, axis=1)


def unpack_kernel(*refs):
    rows_ref = refs[-1]
    _, size, lanes = refs[0].shape
    pack = rows_ref.shape[0] // size
    span = lanes // pack
    for q in range(pack):
        found = [ref[0, :, q * span : (q + 1) * span] for ref in refs[:-1]]
        rows_ref[q * size : (q + 1) * size, :] = jnp.concatenate(found, axis=1)


def packed_trace(rows, batches, pack, size):
    groups = rows.shape[0] // (pack * size)
    return pl.pallas_call(
        pack_kernel,
        grid=(groups,),
        in_specs=[pl.BlockSpec((pack * size, rows.shape[1]), lambda i: (i, 0))],
        out_specs=pl.BlockSpec((batches, 1, size, LANES), lambda i: (0, i, 0, 0)),
        out_shape=jax.ShapeDtypeStruct((batches, groups, size, LANES), rows.dtype),
        compiler_params=pltpu.CompilerParams(vmem_limit_bytes=VMEM_BYTES),
        name="pack_trace",
    )(rows)


def unpacked_trace(packed, pack):
    groups, size, lanes = packed[0].shape
    columns = len(packed) * (lanes // pack)
    return pl.pallas_call(
        unpack_kernel,
        grid=(groups,),
        in_specs=[pl.BlockSpec((1, size, lanes), lambda i: (i, 0, 0))] * len(packed),
        out_specs=pl.BlockSpec((pack * size, columns), lambda i: (i, 0)),
        out_shape=jax.ShapeDtypeStruct((groups * pack * size, columns), jnp.float32),
        compiler_params=pltpu.CompilerParams(vmem_limit_bytes=VMEM_BYTES),
        name="unpack_trace",
    )(*packed)


def in_hbm(array):
    return pltpu.with_memory_space_constraint(array, pltpu.HBM)


def half_kernel(place_ref, values_ref, *refs):
    refs[-1][...] = values_ref[...]


def other_half(values, place, after):
    rows = values.shape[0] // 2
    step = divisor_up_to(rows, 3)
    block = (step,) + values.shape[1:]
    spec = pltpu.PrefetchScalarGridSpec(
        num_scalar_prefetch=1,
        grid=(rows // step,),
        in_specs=[
            pl.BlockSpec(block, lambda i, place_ref: ((1 - place_ref[0]) * (rows // step) + i, 0, 0, 0)),
            pl.BlockSpec(memory_space=pl.ANY),
        ],
        out_specs=pl.BlockSpec(block, lambda i, place_ref: (i, 0, 0, 0)),
    )
    return pl.pallas_call(
        half_kernel,
        grid_spec=spec,
        out_shape=jax.ShapeDtypeStruct((rows,) + values.shape[1:], values.dtype),
        compiler_params=pltpu.CompilerParams(vmem_limit_bytes=VMEM_BYTES),
        name="other_half",
    )(place, values, after)


def split_kernel(place_ref, own_ref, other_ref, *refs):
    parts_ref = refs[-1]
    picks, size = own_ref.shape[1:3]
    for start, values_ref in ((0, own_ref), (picks, other_ref)):
        for k in range(picks):
            value = values_ref[0, k]
            high = value.astype(jnp.bfloat16)
            parts_ref[0, start + k, :size] = high
            parts_ref[0, start + k, size:] = (value - high.astype(jnp.float32)).astype(jnp.bfloat16)


def split_operator(values, other, place, after):
    _, picks, size, depth = values.shape
    rows = other.shape[0]
    spec = pltpu.PrefetchScalarGridSpec(
        num_scalar_prefetch=1,
        grid=(rows,),
        in_specs=[
            pl.BlockSpec((1, picks, size, depth), lambda i, place_ref: (place_ref[0] * rows + i, 0, 0, 0)),
            pl.BlockSpec((1, picks, size, depth), lambda i, place_ref: (i, 0, 0, 0)),
            pl.BlockSpec(memory_space=pltpu.HBM),
        ],
        out_specs=pl.BlockSpec((1, 2 * picks, 2 * size, depth), lambda i, place_ref: (i, 0, 0, 0)),
    )
    return pl.pallas_call(
        split_kernel,
        grid_spec=spec,
        out_shape=jax.ShapeDtypeStruct((rows, 2 * picks, 2 * size, depth), jnp.bfloat16),
        compiler_params=pltpu.CompilerParams(vmem_limit_bytes=VMEM_BYTES),
        name="split_operator",
    )(place, values, other, in_hbm(after))


def apply_kernel(pack, index_ref, parts_ref, gathered_ref, *refs):
    result_ref, token_ref, slots, tiles, arrived = refs[-5:]
    row, rows = pl.program_id(0), pl.num_programs(0)
    count, picks, twice, _ = slots.shape
    size = twice // 2
    pieces, halves, groups, _, lanes = gathered_ref.shape
    span = lanes // pack

    def fetch(which):
        slot = lax.rem(which, count)
        return pltpu.make_async_copy(parts_ref.at[which], slots.at[slot], arrived.at[slot])

    @pl.when(row == 0)
    def _():
        for ahead in range(min(count - 1, parts_ref.shape[0])):
            fetch(ahead).start()

    @pl.when(row + count - 1 < rows)
    def _():
        fetch(row + count - 1).start()

    @pl.when(row == 0)
    def _():
        token_ref[...] = jnp.zeros_like(token_ref)
        lane = lax.broadcasted_iota(jnp.int32, (size, lanes), 1)
        left = lane < lanes // 2
        masks = [lane // span % max(1, pack // 2) == q for q in range(pack // 2)]
        for half in range(halves):
            for piece in range(pieces):
                for group in range(groups):
                    tile = gathered_ref[piece, half, group]
                    high = tile.astype(jnp.bfloat16).astype(jnp.float32)
                    low = tile - high
                    base = ((half * pieces + piece) * groups + group) * pack
                    if pack == 1:
                        tiles[base] = jnp.concatenate([high, low], axis=1).astype(jnp.bfloat16)
                        continue
                    first = jnp.where(left, high, pltpu.roll(low, lanes // 2, 1))
                    second = jnp.where(left, pltpu.roll(high, lanes // 2, 1), low)
                    for start, both in ((base, first), (base + pack // 2, second)):
                        for q, mask in enumerate(masks):
                            alone = both if pack == 2 else jnp.where(mask, both, 0.0)
                            tiles[start + q] = alone.astype(jnp.bfloat16)

    fetch(row).wait()
    slot = lax.rem(row, count)
    picked = jnp.concatenate([tiles[index_ref[row * picks + k]] for k in range(picks)], axis=0)
    block = jnp.concatenate([slots[slot, k] for k in range(picks)], axis=1)
    product = jnp.dot(block, picked, preferred_element_type=jnp.float32)
    total = product[:size] + product[size:]
    if pack == 1:
        result_ref[0] = total[:, :lanes] + total[:, lanes:]
    else:
        shift = span
        while shift < lanes:
            total = total + pltpu.roll(total, shift, 1)
            shift *= 2
        lane = lax.broadcasted_iota(jnp.int32, total.shape, 1)
        result_ref[0] = jnp.where(lane < lax.rem(row, pack) * span, result_ref[0], total)


def apply_operator(parts, index, pack, gathered, after):
    rows, picks, twice, depth = parts.shape
    pieces, halves, groups, size, lanes = gathered.shape
    spec = pltpu.PrefetchScalarGridSpec(
        num_scalar_prefetch=1,
        grid=(rows,),
        in_specs=[
            pl.BlockSpec(memory_space=pltpu.HBM),
            pl.BlockSpec(gathered.shape, lambda row, *_: (0, 0, 0, 0, 0)),
        ]
        + [pl.BlockSpec(memory_space=pl.ANY)] * len(after),
        out_specs=[pl.BlockSpec((1, size, lanes), lambda row, *_: (row // pack, 0, 0)), TOKEN_SPEC],
        scratch_shapes=[
            pltpu.VMEM((SLOTS, picks, twice, depth), jnp.bfloat16),
            pltpu.VMEM((halves * pieces * groups * pack, size, lanes * (2 if pack == 1 else 1)), jnp.bfloat16),
            pltpu.SemaphoreType.DMA((SLOTS,)),
        ],
    )

    def kernel(*refs):
        apply_kernel(pack, *refs)

    return pl.pallas_call(
        kernel,
        grid_spec=spec,
        out_shape=[jax.ShapeDtypeStruct((groups, size, lanes), jnp.float32), TOKEN],
        compiler_params=pltpu.CompilerParams(vmem_limit_bytes=VMEM_BYTES),
        cost_estimate=pl.CostEstimate(flops=0, bytes_accessed=gathered.size, transcendentals=0),
        name="apply_operator",
    )(index, in_hbm(parts), in_hbm(gathered), *after)


def sum_kernel(terms, *refs):
    total_ref, token_ref = refs[-2:]
    total_ref[...] = sum(ref[...] for ref in refs[:terms])
    token_ref[...] = jnp.zeros_like(token_ref)


def sum_of(terms, after):
    shape = terms[0].shape
    whole = pl.BlockSpec(shape, lambda i: (0, 0, 0))

    def kernel(*refs):
        sum_kernel(len(terms), *refs)

    return pl.pallas_call(
        kernel,
        grid=(1,),
        in_specs=[whole] * len(terms) + [pl.BlockSpec(memory_space=pl.ANY)] * len(after),
        out_specs=[whole, TOKEN_SPEC],
        out_shape=[jax.ShapeDtypeStruct(shape, jnp.float32), TOKEN],
        compiler_params=pltpu.CompilerParams(vmem_limit_bytes=VMEM_BYTES),
        name="sum_of",
    )(*terms, *after)


def shards(sources, tr_vals, tr_cols, rf_vals, rf_cols):
    source = sources[0, 0, 0]
    piece_rows, columns = source.shape
    size = tr_vals.shape[-1]
    blocks = piece_rows // size
    pack = 4 if blocks % 4 == 0 else 1
    batches, delay = columns // (LANES // pack), DELAY
    length, pieces = lax.axis_size("slab"), lax.axis_size("col")
    last = length - 1
    position = lax.axis_index("slab")
    place = lax.axis_index("row")
    swap = [(0, 1), (1, 0)]
    source = packed_trace(source, batches, pack, size)

    def operator(values, columns, copy_after, split_after):
        half = values.shape[0] // 2
        own = lax.dynamic_slice_in_dim(columns, place * half, half, 0)
        other = lax.dynamic_slice_in_dim(columns, (1 - place) * half, half, 0)
        group_blocks = pieces * blocks
        other = lax.ppermute(other, "row", swap) + (1 - place) * group_blocks
        index = jnp.concatenate([own + place * group_blocks, other], axis=1)
        traded = lax.ppermute(other_half(values, place.reshape(1), copy_after), "row", swap)
        return split_operator(values, traded, place.reshape(1), split_after), index.reshape(-1), pack

    def by_position(choices):
        known = [choice for choice in choices if choice is not None]
        chosen = known[-1]
        for slab, choice in enumerate(choices):
            if choice is not None and choice is not chosen:
                chosen = jnp.where(position == slab, choice, chosen)
        return chosen

    def held(results, batch_of, shift):
        return by_position(
            [
                results[batch_of(slab) + shift(slab)] if 0 <= batch_of(slab) < batches else None
                for slab in range(length)
            ]
        )

    def gather(piece):
        gathered = lax.all_gather(piece, ("col", "row"), axis=0)
        return gathered.reshape((pieces, 2) + piece.shape)

    moments = batches + delay * last
    downs, refls, ups, tokens = [], [], [], []

    def incident_of(moment):
        after = tokens[moment - delay : moment - delay + 1]
        if moment < moments:
            which = jnp.clip(moment - delay * position, 0, batches - 1)
            terms = [lax.dynamic_index_in_dim(source, which, 0, keepdims=False)]
            if moment >= delay:
                terms.append(passed_along(downs[moment - delay], "slab", 1))
        else:
            at = moment - moments
            terms = [held(refls, lambda slab: at - delay * (last - slab), lambda slab: delay * slab)]
            if at >= delay:
                terms.append(passed_along(ups[at - delay], "slab", -1))
        return sum_of(terms, after)

    piece, _ = incident_of(0)
    gathered = [gather(piece)]
    trans = operator(tr_vals[0, 0, 0], tr_cols[0, 0, 0], piece, gathered[0])
    lag = max(0, min(delay, batches - 2))
    copied_after = piece
    for moment in range(2 * moments):
        after = tokens[-1:]
        if moment + 1 < 2 * moments:
            piece, token = incident_of(moment + 1)
            gathered.append(gather(piece))
            after = after + [token]
        if moment == 0:
            after = after + [in_hbm(gathered[1])]
        product, token = apply_operator(*trans, gathered[moment], after)
        (downs if moment < moments else ups).append(product)
        if moment == max(0, lag - 1):
            refl = operator(rf_vals[0, 0, 0], rf_cols[0, 0, 0], copied_after, token)
        if lag <= moment < moments + lag:
            product, token = apply_operator(*refl, gathered[moment - lag], [token])
            refls.append(product)
        tokens.append(token)
    totals = [
        held(downs, lambda slab: batch, lambda slab: delay * slab)
        + held(ups, lambda slab: batch, lambda slab: delay * (last - slab))
        for batch in range(batches)
    ]
    return unpacked_trace(totals, pack)[None, None, None]


def solution(mesh):
    placed = (
        P("slab", "col", "row", None, None),
        P("slab", "col", "row", None, None, None, None),
        P("slab", "col", "row", None, None),
        P("slab", "col", "row", None, None, None, None),
        P("slab", "col", "row", None, None),
    )
    return jax.shard_map(
        shards,
        mesh=mesh,
        in_specs=placed,
        out_specs=P("slab", "col", "row", None, None),
        check_vma=False,
    )
```

```python
import jax
import jax.numpy as jnp
from jax import lax
from jax.experimental import pallas as pl
from jax.experimental.pallas import tpu as pltpu
from jax.sharding import PartitionSpec as P

LANES = 128
DELAY = 2
SLOTS = 8
VMEM_BYTES = 44 * 2**20
TOKEN = jax.ShapeDtypeStruct((8, LANES), jnp.float32)
TOKEN_SPEC = pl.BlockSpec(TOKEN.shape, lambda *_: (0, 0))


def divisor_up_to(number, limit):
    return max(n for n in range(1, limit + 1) if number % n == 0)


def passed_along(value, axis, steps):
    count = lax.axis_size(axis)
    initial, last = (max(0, -steps), min(count, count - steps))
    return lax.ppermute(value, axis, [(source, source + steps) for source in range(initial, last)])


def pack_kernel(rows_ref, packed_ref):
    batches, _, size, lanes = packed_ref.shape
    pack = rows_ref.shape[0] // size
    span = lanes // pack
    for batch in range(batches):
        found = [rows_ref[q * size : (q + 1) * size, batch * span : (batch + 1) * span] for q in range(pack)]
        packed_ref[batch, 0] = jnp.concatenate(found, axis=1)


def unpack_kernel(*refs):
    rows_ref = refs[-1]
    _, size, lanes = refs[0].shape
    pack = rows_ref.shape[0] // size
    span = lanes // pack
    for q in range(pack):
        found = [ref[0, :, q * span : (q + 1) * span] for ref in refs[:-1]]
        rows_ref[q * size : (q + 1) * size, :] = jnp.concatenate(found, axis=1)


def packed_trace(rows, batches, pack, size):
    groups = rows.shape[0] // (pack * size)
    return pl.pallas_call(
        pack_kernel,
        grid=(groups,),
        in_specs=[pl.BlockSpec((pack * size, rows.shape[1]), lambda i: (i, 0))],
        out_specs=pl.BlockSpec((batches, 1, size, LANES), lambda i: (0, i, 0, 0)),
        out_shape=jax.ShapeDtypeStruct((batches, groups, size, LANES), rows.dtype),
        compiler_params=pltpu.CompilerParams(vmem_limit_bytes=VMEM_BYTES),
        name="pack_trace",
    )(rows)


def unpacked_trace(packed, pack):
    groups, size, lanes = packed[0].shape
    columns = len(packed) * (lanes // pack)
    return pl.pallas_call(
        unpack_kernel,
        grid=(groups,),
        in_specs=[pl.BlockSpec((1, size, lanes), lambda i: (i, 0, 0))] * len(packed),
        out_specs=pl.BlockSpec((pack * size, columns), lambda i: (i, 0)),
        out_shape=jax.ShapeDtypeStruct((groups * pack * size, columns), jnp.float32),
        compiler_params=pltpu.CompilerParams(vmem_limit_bytes=VMEM_BYTES),
        name="unpack_trace",
    )(*packed)


def in_hbm(array):
    return pltpu.with_memory_space_constraint(array, pltpu.HBM)


def half_kernel(place_ref, values_ref, *refs):
    refs[-1][...] = values_ref[...]


def other_half(values, place, after):
    rows = values.shape[0] // 2
    step = divisor_up_to(rows, 3)
    block = (step,) + values.shape[1:]
    spec = pltpu.PrefetchScalarGridSpec(
        num_scalar_prefetch=1,
        grid=(rows // step,),
        in_specs=[
            pl.BlockSpec(block, lambda i, place_ref: ((1 - place_ref[0]) * (rows // step) + i, 0, 0, 0)),
            pl.BlockSpec(memory_space=pl.ANY),
        ],
        out_specs=pl.BlockSpec(block, lambda i, place_ref: (i, 0, 0, 0)),
    )
    return pl.pallas_call(
        half_kernel,
        grid_spec=spec,
        out_shape=jax.ShapeDtypeStruct((rows,) + values.shape[1:], values.dtype),
        compiler_params=pltpu.CompilerParams(vmem_limit_bytes=VMEM_BYTES),
        name="other_half",
    )(place, values, after)


def split_kernel(place_ref, own_ref, other_ref, *refs):
    parts_ref = refs[-1]
    picks, size = own_ref.shape[1:3]
    for start, values_ref in ((0, own_ref), (picks, other_ref)):
        for k in range(picks):
            value = values_ref[0, k]
            high = value.astype(jnp.bfloat16)
            parts_ref[0, start + k, :size] = high
            parts_ref[0, start + k, size:] = (value - high.astype(jnp.float32)).astype(jnp.bfloat16)


def split_operator(values, other, place, after):
    _, picks, size, depth = values.shape
    rows = other.shape[0]
    spec = pltpu.PrefetchScalarGridSpec(
        num_scalar_prefetch=1,
        grid=(rows,),
        in_specs=[
            pl.BlockSpec((1, picks, size, depth), lambda i, place_ref: (place_ref[0] * rows + i, 0, 0, 0)),
            pl.BlockSpec((1, picks, size, depth), lambda i, place_ref: (i, 0, 0, 0)),
            pl.BlockSpec(memory_space=pltpu.HBM),
        ],
        out_specs=pl.BlockSpec((1, 2 * picks, 2 * size, depth), lambda i, place_ref: (i, 0, 0, 0)),
    )
    return pl.pallas_call(
        split_kernel,
        grid_spec=spec,
        out_shape=jax.ShapeDtypeStruct((rows, 2 * picks, 2 * size, depth), jnp.bfloat16),
        compiler_params=pltpu.CompilerParams(vmem_limit_bytes=VMEM_BYTES),
        name="split_operator",
    )(place, values, other, in_hbm(after))


def apply_kernel(pack, index_ref, parts_ref, gathered_ref, *refs):
    result_ref, token_ref, slots, tiles, arrived = refs[-5:]
    row, rows = pl.program_id(0), pl.num_programs(0)
    count, picks, twice, _ = slots.shape
    size = twice // 2
    pieces, halves, groups, _, lanes = gathered_ref.shape
    span = lanes // pack

    def fetch(which):
        slot = lax.rem(which, count)
        return pltpu.make_async_copy(parts_ref.at[which], slots.at[slot], arrived.at[slot])

    @pl.when(row == 0)
    def _():
        for ahead in range(min(count - 1, parts_ref.shape[0])):
            fetch(ahead).start()

    @pl.when(row + count - 1 < rows)
    def _():
        fetch(row + count - 1).start()

    @pl.when(row == 0)
    def _():
        token_ref[...] = jnp.zeros_like(token_ref)
        middle = lanes // 2
        lane = lax.broadcasted_iota(jnp.int32, (size, lanes), 1) // span % max(1, pack // 2)
        masks = [(lane == q).astype(jnp.float32).astype(jnp.bfloat16) for q in range(pack // 2)]
        for half in range(halves):
            for piece in range(pieces):
                for group in range(groups):
                    tile = gathered_ref[piece, half, group]
                    high = tile.astype(jnp.bfloat16)
                    low = (tile - high.astype(jnp.float32)).astype(jnp.bfloat16)
                    base = ((half * pieces + piece) * groups + group) * pack
                    if pack == 1:
                        tiles[base] = jnp.concatenate([high, low], axis=1)
                        continue
                    first = jnp.concatenate([high[:, :middle], low[:, :middle]], axis=1)
                    second = jnp.concatenate([high[:, middle:], low[:, middle:]], axis=1)
                    for start, both in ((base, first), (base + pack // 2, second)):
                        for q, mask in enumerate(masks):
                            tiles[start + q] = both if pack == 2 else both * mask

    fetch(row).wait()
    slot = lax.rem(row, count)
    picked = jnp.concatenate([tiles[index_ref[row * picks + k]] for k in range(picks)], axis=0)
    block = jnp.concatenate([slots[slot, k] for k in range(picks)], axis=1)
    product = jnp.dot(block, picked, preferred_element_type=jnp.float32)
    total = product[:size] + product[size:]
    if pack == 1:
        result_ref[0] = total[:, :lanes] + total[:, lanes:]
    else:
        shift = span
        while shift < lanes:
            total = total + pltpu.roll(total, shift, 1)
            shift *= 2
        lane = lax.broadcasted_iota(jnp.int32, total.shape, 1)
        result_ref[0] = jnp.where(lane < lax.rem(row, pack) * span, result_ref[0], total)


def apply_operator(parts, index, pack, gathered, after):
    rows, picks, twice, depth = parts.shape
    pieces, halves, groups, size, lanes = gathered.shape
    spec = pltpu.PrefetchScalarGridSpec(
        num_scalar_prefetch=1,
        grid=(rows,),
        in_specs=[
            pl.BlockSpec(memory_space=pltpu.HBM),
            pl.BlockSpec(gathered.shape, lambda row, *_: (0, 0, 0, 0, 0)),
        ]
        + [pl.BlockSpec(memory_space=pl.ANY)] * len(after),
        out_specs=[pl.BlockSpec((1, size, lanes), lambda row, *_: (row // pack, 0, 0)), TOKEN_SPEC],
        scratch_shapes=[
            pltpu.VMEM((SLOTS, picks, twice, depth), jnp.bfloat16),
            pltpu.VMEM((halves * pieces * groups * pack, size, lanes * (2 if pack == 1 else 1)), jnp.bfloat16),
            pltpu.SemaphoreType.DMA((SLOTS,)),
        ],
    )

    def kernel(*refs):
        apply_kernel(pack, *refs)

    return pl.pallas_call(
        kernel,
        grid_spec=spec,
        out_shape=[jax.ShapeDtypeStruct((groups, size, lanes), jnp.float32), TOKEN],
        compiler_params=pltpu.CompilerParams(vmem_limit_bytes=VMEM_BYTES),
        cost_estimate=pl.CostEstimate(flops=0, bytes_accessed=gathered.size, transcendentals=0),
        name="apply_operator",
    )(index, in_hbm(parts), in_hbm(gathered), *after)


def sum_kernel(terms, *refs):
    total_ref, token_ref = refs[-2:]
    total_ref[...] = sum(ref[...] for ref in refs[:terms])
    token_ref[...] = jnp.zeros_like(token_ref)


def sum_of(terms, after):
    shape = terms[0].shape
    whole = pl.BlockSpec(shape, lambda i: (0, 0, 0))

    def kernel(*refs):
        sum_kernel(len(terms), *refs)

    return pl.pallas_call(
        kernel,
        grid=(1,),
        in_specs=[whole] * len(terms) + [pl.BlockSpec(memory_space=pl.ANY)] * len(after),
        out_specs=[whole, TOKEN_SPEC],
        out_shape=[jax.ShapeDtypeStruct(shape, jnp.float32), TOKEN],
        compiler_params=pltpu.CompilerParams(vmem_limit_bytes=VMEM_BYTES),
        name="sum_of",
    )(*terms, *after)


def shards(sources, tr_vals, tr_cols, rf_vals, rf_cols):
    source = sources[0, 0, 0]
    piece_rows, columns = source.shape
    size = tr_vals.shape[-1]
    blocks = piece_rows // size
    pack = 4 if blocks % 4 == 0 else 1
    batches, delay = columns // (LANES // pack), DELAY
    length, pieces = lax.axis_size("slab"), lax.axis_size("col")
    last = length - 1
    position = lax.axis_index("slab")
    place = lax.axis_index("row")
    swap = [(0, 1), (1, 0)]
    source = packed_trace(source, batches, pack, size)

    def operator(values, columns, copy_after, split_after):
        half = values.shape[0] // 2
        own = lax.dynamic_slice_in_dim(columns, place * half, half, 0)
        other = lax.dynamic_slice_in_dim(columns, (1 - place) * half, half, 0)
        group_blocks = pieces * blocks
        other = lax.ppermute(other, "row", swap) + (1 - place) * group_blocks
        index = jnp.concatenate([own + place * group_blocks, other], axis=1)
        traded = lax.ppermute(other_half(values, place.reshape(1), copy_after), "row", swap)
        return split_operator(values, traded, place.reshape(1), split_after), index.reshape(-1), pack

    def by_position(choices):
        known = [choice for choice in choices if choice is not None]
        chosen = known[-1]
        for slab, choice in enumerate(choices):
            if choice is not None and choice is not chosen:
                chosen = jnp.where(position == slab, choice, chosen)
        return chosen

    def held(results, batch_of, shift):
        return by_position(
            [
                results[batch_of(slab) + shift(slab)] if 0 <= batch_of(slab) < batches else None
                for slab in range(length)
            ]
        )

    def gather(piece):
        gathered = lax.all_gather(piece, ("col", "row"), axis=0)
        return gathered.reshape((pieces, 2) + piece.shape)

    moments = batches + delay * last
    downs, refls, ups, tokens = [], [], [], []

    def incident_of(moment, ready=()):
        after = [*tokens[moment - delay : moment - delay + 1], *ready]
        if moment < moments:
            which = jnp.clip(moment - delay * position, 0, batches - 1)
            terms = [lax.dynamic_index_in_dim(source, which, 0, keepdims=False)]
            if moment >= delay:
                terms.append(passed_along(downs[moment - delay], "slab", 1))
        else:
            at = moment - moments
            terms = [held(refls, lambda slab: at - delay * (last - slab), lambda slab: delay * slab)]
            if at >= delay:
                terms.append(passed_along(ups[at - delay], "slab", -1))
        return sum_of(terms, after)

    piece, _ = incident_of(0)
    gathered = [gather(piece)]
    trans = operator(tr_vals[0, 0, 0], tr_cols[0, 0, 0], piece, gathered[0])
    lag = max(0, min(delay, batches - 2))
    copied_after, ready = in_hbm(gathered[0]), []
    for moment in range(2 * moments):
        after = tokens[-1:]
        if moment + 1 < 2 * moments:
            piece, token = incident_of(moment + 1, ready if moment == lag else [])
            gathered.append(gather(piece))
            after = after + [token]
        if moment == 0:
            after = after + [in_hbm(gathered[1])]
        product, token = apply_operator(*trans, gathered[moment], after)
        (downs if moment < moments else ups).append(product)
        if moment == max(0, lag - 1):
            refl = operator(rf_vals[0, 0, 0], rf_cols[0, 0, 0], copied_after, token)
            ready = [in_hbm(refl[0])]
        if lag <= moment < moments + lag:
            product, token = apply_operator(*refl, gathered[moment - lag], [token])
            refls.append(product)
        tokens.append(token)
    totals = [
        held(downs, lambda slab: batch, lambda slab: delay * slab)
        + held(ups, lambda slab: batch, lambda slab: delay * (last - slab))
        for batch in range(batches)
    ]
    return unpacked_trace(totals, pack)[None, None, None]


def solution(mesh):
    placed = (
        P("slab", "col", "row", None, None),
        P("slab", "col", "row", None, None, None, None),
        P("slab", "col", "row", None, None),
        P("slab", "col", "row", None, None, None, None),
        P("slab", "col", "row", None, None),
    )
    return jax.shard_map(
        shards,
        mesh=mesh,
        in_specs=placed,
        out_specs=P("slab", "col", "row", None, None),
        check_vma=False,
    )
```

```python
import jax
import jax.numpy as jnp
from jax import lax
from jax.experimental import pallas as pl
from jax.experimental.pallas import tpu as pltpu
from jax.sharding import PartitionSpec as P

LANES = 128
DELAY = 2
SLOTS = 8
VMEM_BYTES = 44 * 2**20
TOKEN = jax.ShapeDtypeStruct((8, LANES), jnp.float32)
TOKEN_SPEC = pl.BlockSpec(TOKEN.shape, lambda *_: (0, 0))


def divisor_up_to(number, limit):
    return max(n for n in range(1, limit + 1) if number % n == 0)


def passed_along(value, axis, steps):
    count = lax.axis_size(axis)
    initial, last = (max(0, -steps), min(count, count - steps))
    return lax.ppermute(value, axis, [(source, source + steps) for source in range(initial, last)])


def pack_kernel(rows_ref, packed_ref):
    batches, _, size, lanes = packed_ref.shape
    pack = rows_ref.shape[0] // size
    span = lanes // pack
    for batch in range(batches):
        found = [rows_ref[q * size : (q + 1) * size, batch * span : (batch + 1) * span] for q in range(pack)]
        packed_ref[batch, 0] = jnp.concatenate(found, axis=1)


def unpack_kernel(*refs):
    rows_ref = refs[-1]
    _, size, lanes = refs[0].shape
    pack = rows_ref.shape[0] // size
    span = lanes // pack
    for q in range(pack):
        found = [ref[0, :, q * span : (q + 1) * span] for ref in refs[:-1]]
        rows_ref[q * size : (q + 1) * size, :] = jnp.concatenate(found, axis=1)


def packed_trace(rows, batches, pack, size):
    groups = rows.shape[0] // (pack * size)
    return pl.pallas_call(
        pack_kernel,
        grid=(groups,),
        in_specs=[pl.BlockSpec((pack * size, rows.shape[1]), lambda i: (i, 0))],
        out_specs=pl.BlockSpec((batches, 1, size, LANES), lambda i: (0, i, 0, 0)),
        out_shape=jax.ShapeDtypeStruct((batches, groups, size, LANES), rows.dtype),
        compiler_params=pltpu.CompilerParams(vmem_limit_bytes=VMEM_BYTES),
        name="pack_trace",
    )(rows)


def unpacked_trace(packed, pack):
    groups, size, lanes = packed[0].shape
    columns = len(packed) * (lanes // pack)
    return pl.pallas_call(
        unpack_kernel,
        grid=(groups,),
        in_specs=[pl.BlockSpec((1, size, lanes), lambda i: (i, 0, 0))] * len(packed),
        out_specs=pl.BlockSpec((pack * size, columns), lambda i: (i, 0)),
        out_shape=jax.ShapeDtypeStruct((groups * pack * size, columns), jnp.float32),
        compiler_params=pltpu.CompilerParams(vmem_limit_bytes=VMEM_BYTES),
        name="unpack_trace",
    )(*packed)


def in_hbm(array):
    return pltpu.with_memory_space_constraint(array, pltpu.HBM)


def half_kernel(place_ref, values_ref, *refs):
    refs[-1][...] = values_ref[...]


def other_half(values, place, after):
    rows = values.shape[0] // 2
    step = divisor_up_to(rows, 3)
    block = (step,) + values.shape[1:]
    spec = pltpu.PrefetchScalarGridSpec(
        num_scalar_prefetch=1,
        grid=(rows // step,),
        in_specs=[
            pl.BlockSpec(block, lambda i, place_ref: ((1 - place_ref[0]) * (rows // step) + i, 0, 0, 0)),
            pl.BlockSpec(memory_space=pl.ANY),
        ],
        out_specs=pl.BlockSpec(block, lambda i, place_ref: (i, 0, 0, 0)),
    )
    return pl.pallas_call(
        half_kernel,
        grid_spec=spec,
        out_shape=jax.ShapeDtypeStruct((rows,) + values.shape[1:], values.dtype),
        compiler_params=pltpu.CompilerParams(vmem_limit_bytes=VMEM_BYTES),
        name="other_half",
    )(place, values, after)


def split_kernel(place_ref, own_ref, other_ref, *refs):
    parts_ref = refs[-1]
    picks, size = own_ref.shape[1:3]
    for start, values_ref in ((0, own_ref), (picks, other_ref)):
        for k in range(picks):
            value = values_ref[0, k]
            high = value.astype(jnp.bfloat16)
            parts_ref[0, start + k, :size] = high
            parts_ref[0, start + k, size:] = (value - high.astype(jnp.float32)).astype(jnp.bfloat16)


def split_operator(values, other, place, after):
    _, picks, size, depth = values.shape
    rows = other.shape[0]
    spec = pltpu.PrefetchScalarGridSpec(
        num_scalar_prefetch=1,
        grid=(rows,),
        in_specs=[
            pl.BlockSpec((1, picks, size, depth), lambda i, place_ref: (place_ref[0] * rows + i, 0, 0, 0)),
            pl.BlockSpec((1, picks, size, depth), lambda i, place_ref: (i, 0, 0, 0)),
            pl.BlockSpec(memory_space=pltpu.HBM),
        ],
        out_specs=pl.BlockSpec((1, 2 * picks, 2 * size, depth), lambda i, place_ref: (i, 0, 0, 0)),
    )
    return pl.pallas_call(
        split_kernel,
        grid_spec=spec,
        out_shape=jax.ShapeDtypeStruct((rows, 2 * picks, 2 * size, depth), jnp.bfloat16),
        compiler_params=pltpu.CompilerParams(vmem_limit_bytes=VMEM_BYTES),
        name="split_operator",
    )(place, values, other, in_hbm(after))


def apply_kernel(pack, index_ref, parts_ref, gathered_ref, *refs):
    result_ref, token_ref, slots, tiles, held, arrived, landed = refs[-7:]
    row, rows = pl.program_id(0), pl.num_programs(0)
    count, picks, twice, _ = slots.shape
    size = twice // 2
    pieces, halves, groups, _, lanes = gathered_ref.shape
    span = lanes // pack

    class Copies:
        def __init__(self, source, target, signals):
            cut = source.shape[0] // 2
            ends = ((0, cut), (cut, source.shape[0] - cut))
            self.halves = [
                pltpu.make_async_copy(source.at[pl.ds(*end)], target.at[pl.ds(*end)], signal)
                for end, signal in zip(ends, signals)
            ]

        def start(self):
            for priority, half in enumerate(self.halves):
                half.start(priority=priority)

        def wait(self):
            for half in self.halves:
                half.wait()

    def fetch(which):
        slot = lax.rem(which, count)
        signals = [arrived.at[slot, part] for part in range(2)]
        return Copies(parts_ref.at[which], slots.at[slot], signals)

    pieces_here = Copies(gathered_ref, held, [landed.at[part] for part in range(2)])

    @pl.when(row == 0)
    def _():
        pieces_here.start()
        for ahead in range(min(count - 1, parts_ref.shape[0])):
            fetch(ahead).start()

    @pl.when(row + count - 1 < rows)
    def _():
        fetch(row + count - 1).start()

    @pl.when(row == 0)
    def _():
        token_ref[...] = jnp.zeros_like(token_ref)
        pieces_here.wait()
        middle = lanes // 2
        lane = lax.broadcasted_iota(jnp.int32, (size, lanes), 1) // span % max(1, pack // 2)
        masks = [(lane == q).astype(jnp.float32).astype(jnp.bfloat16) for q in range(pack // 2)]
        for half in range(halves):
            for piece in range(pieces):
                for group in range(groups):
                    tile = held[piece, half, group]
                    high = tile.astype(jnp.bfloat16)
                    low = (tile - high.astype(jnp.float32)).astype(jnp.bfloat16)
                    base = ((half * pieces + piece) * groups + group) * pack
                    if pack == 1:
                        tiles[base] = jnp.concatenate([high, low], axis=1)
                        continue
                    first = jnp.concatenate([high[:, :middle], low[:, :middle]], axis=1)
                    second = jnp.concatenate([high[:, middle:], low[:, middle:]], axis=1)
                    for start, both in ((base, first), (base + pack // 2, second)):
                        for q, mask in enumerate(masks):
                            tiles[start + q] = both if pack == 2 else both * mask

    fetch(row).wait()
    slot = lax.rem(row, count)
    picked = jnp.concatenate([tiles[index_ref[row * picks + k]] for k in range(picks)], axis=0)
    block = jnp.concatenate([slots[slot, k] for k in range(picks)], axis=1)
    product = jnp.dot(block, picked, preferred_element_type=jnp.float32)
    total = product[:size] + product[size:]
    if pack == 1:
        result_ref[0] = total[:, :lanes] + total[:, lanes:]
    else:
        shift = span
        while shift < lanes:
            total = total + pltpu.roll(total, shift, 1)
            shift *= 2
        lane = lax.broadcasted_iota(jnp.int32, total.shape, 1)
        result_ref[0] = jnp.where(lane < lax.rem(row, pack) * span, result_ref[0], total)


def apply_operator(parts, index, pack, gathered, after):
    rows, picks, twice, depth = parts.shape
    pieces, halves, groups, size, lanes = gathered.shape
    spec = pltpu.PrefetchScalarGridSpec(
        num_scalar_prefetch=1,
        grid=(rows,),
        in_specs=[
            pl.BlockSpec(memory_space=pltpu.HBM),
            pl.BlockSpec(memory_space=pltpu.HBM),
        ]
        + [pl.BlockSpec(memory_space=pl.ANY)] * len(after),
        out_specs=[pl.BlockSpec((1, size, lanes), lambda row, *_: (row // pack, 0, 0)), TOKEN_SPEC],
        scratch_shapes=[
            pltpu.VMEM((SLOTS, picks, twice, depth), jnp.bfloat16),
            pltpu.VMEM((halves * pieces * groups * pack, size, lanes * (2 if pack == 1 else 1)), jnp.bfloat16),
            pltpu.VMEM(gathered.shape, jnp.float32),
            pltpu.SemaphoreType.DMA((SLOTS, 2)),
            pltpu.SemaphoreType.DMA((2,)),
        ],
    )

    def kernel(*refs):
        apply_kernel(pack, *refs)

    return pl.pallas_call(
        kernel,
        grid_spec=spec,
        out_shape=[jax.ShapeDtypeStruct((groups, size, lanes), jnp.float32), TOKEN],
        compiler_params=pltpu.CompilerParams(vmem_limit_bytes=VMEM_BYTES),
        cost_estimate=pl.CostEstimate(flops=0, bytes_accessed=gathered.size, transcendentals=0),
        name="apply_operator",
    )(index, in_hbm(parts), in_hbm(gathered), *after)


def sum_kernel(terms, *refs):
    total_ref, token_ref = refs[-2:]
    total_ref[...] = sum(ref[...] for ref in refs[:terms])
    token_ref[...] = jnp.zeros_like(token_ref)


def sum_of(terms, after):
    shape = terms[0].shape
    whole = pl.BlockSpec(shape, lambda i: (0, 0, 0))

    def kernel(*refs):
        sum_kernel(len(terms), *refs)

    return pl.pallas_call(
        kernel,
        grid=(1,),
        in_specs=[whole] * len(terms) + [pl.BlockSpec(memory_space=pl.ANY)] * len(after),
        out_specs=[whole, TOKEN_SPEC],
        out_shape=[jax.ShapeDtypeStruct(shape, jnp.float32), TOKEN],
        compiler_params=pltpu.CompilerParams(vmem_limit_bytes=VMEM_BYTES),
        name="sum_of",
    )(*terms, *after)


def shards(sources, tr_vals, tr_cols, rf_vals, rf_cols):
    source = sources[0, 0, 0]
    piece_rows, columns = source.shape
    size = tr_vals.shape[-1]
    blocks = piece_rows // size
    pack = 4 if blocks % 4 == 0 else 1
    batches, delay = columns // (LANES // pack), DELAY
    length, pieces = lax.axis_size("slab"), lax.axis_size("col")
    last = length - 1
    position = lax.axis_index("slab")
    place = lax.axis_index("row")
    swap = [(0, 1), (1, 0)]
    source = packed_trace(source, batches, pack, size)

    def operator(values, columns, copy_after, split_after):
        half = values.shape[0] // 2
        own = lax.dynamic_slice_in_dim(columns, place * half, half, 0)
        other = lax.dynamic_slice_in_dim(columns, (1 - place) * half, half, 0)
        group_blocks = pieces * blocks
        other = lax.ppermute(other, "row", swap) + (1 - place) * group_blocks
        index = jnp.concatenate([own + place * group_blocks, other], axis=1)
        traded = lax.ppermute(other_half(values, place.reshape(1), copy_after), "row", swap)
        return split_operator(values, traded, place.reshape(1), split_after), index.reshape(-1), pack

    def by_position(choices):
        known = [choice for choice in choices if choice is not None]
        chosen = known[-1]
        for slab, choice in enumerate(choices):
            if choice is not None and choice is not chosen:
                chosen = jnp.where(position == slab, choice, chosen)
        return chosen

    def held(results, batch_of, shift):
        return by_position(
            [
                results[batch_of(slab) + shift(slab)] if 0 <= batch_of(slab) < batches else None
                for slab in range(length)
            ]
        )

    def gather(piece):
        gathered = lax.all_gather(piece, ("col", "row"), axis=0)
        return gathered.reshape((pieces, 2) + piece.shape)

    moments = batches + delay * last
    downs, refls, ups, tokens = [], [], [], []

    def incident_of(moment, ready=()):
        after = [*tokens[moment - delay : moment - delay + 1], *ready]
        if moment < moments:
            which = jnp.clip(moment - delay * position, 0, batches - 1)
            terms = [lax.dynamic_index_in_dim(source, which, 0, keepdims=False)]
            if moment >= delay:
                terms.append(passed_along(downs[moment - delay], "slab", 1))
        else:
            at = moment - moments
            terms = [held(refls, lambda slab: at - delay * (last - slab), lambda slab: delay * slab)]
            if at >= delay:
                terms.append(passed_along(ups[at - delay], "slab", -1))
        return sum_of(terms, after)

    piece, _ = incident_of(0)
    gathered = [gather(piece)]
    trans = operator(tr_vals[0, 0, 0], tr_cols[0, 0, 0], piece, gathered[0])
    lag = max(0, min(delay, batches - 2))
    copied_after, ready = in_hbm(gathered[0]), []
    for moment in range(2 * moments):
        after = tokens[-1:]
        if moment + 1 < 2 * moments:
            piece, token = incident_of(moment + 1, ready if moment == lag else [])
            gathered.append(gather(piece))
            after = after + [token]
        if moment == 0:
            after = after + [in_hbm(gathered[1])]
        product, token = apply_operator(*trans, gathered[moment], after)
        (downs if moment < moments else ups).append(product)
        if moment == max(0, lag - 1):
            refl = operator(rf_vals[0, 0, 0], rf_cols[0, 0, 0], copied_after, token)
            ready = [in_hbm(refl[0])]
        if lag <= moment < moments + lag:
            product, token = apply_operator(*refl, gathered[moment - lag], [token])
            refls.append(product)
        tokens.append(token)
    totals = [
        held(downs, lambda slab: batch, lambda slab: delay * slab)
        + held(ups, lambda slab: batch, lambda slab: delay * (last - slab))
        for batch in range(batches)
    ]
    return unpacked_trace(totals, pack)[None, None, None]


def solution(mesh):
    placed = (
        P("slab", "col", "row", None, None),
        P("slab", "col", "row", None, None, None, None),
        P("slab", "col", "row", None, None),
        P("slab", "col", "row", None, None, None, None),
        P("slab", "col", "row", None, None),
    )
    return jax.shard_map(
        shards,
        mesh=mesh,
        in_specs=placed,
        out_specs=P("slab", "col", "row", None, None),
        check_vma=False,
    )
```

```python
import jax
import jax.numpy as jnp
from jax import lax
from jax.experimental import pallas as pl
from jax.experimental.pallas import tpu as pltpu
from jax.sharding import PartitionSpec as P

LANES = 128
DELAY = 2
SLOTS = 8
VMEM_BYTES = 44 * 2**20
TOKEN = jax.ShapeDtypeStruct((8, LANES), jnp.float32)
TOKEN_SPEC = pl.BlockSpec(TOKEN.shape, lambda *_: (0, 0))


def divisor_up_to(number, limit):
    return max(n for n in range(1, limit + 1) if number % n == 0)


def passed_along(value, axis, steps):
    count = lax.axis_size(axis)
    initial, last = (max(0, -steps), min(count, count - steps))
    return lax.ppermute(value, axis, [(source, source + steps) for source in range(initial, last)])


def pack_kernel(rows_ref, packed_ref):
    batches, _, size, lanes = packed_ref.shape
    pack = rows_ref.shape[0] // size
    span = lanes // pack
    for batch in range(batches):
        found = [rows_ref[q * size : (q + 1) * size, batch * span : (batch + 1) * span] for q in range(pack)]
        packed_ref[batch, 0] = jnp.concatenate(found, axis=1)


def unpack_kernel(*refs):
    rows_ref = refs[-1]
    _, size, lanes = refs[0].shape
    pack = rows_ref.shape[0] // size
    span = lanes // pack
    for q in range(pack):
        found = [ref[0, :, q * span : (q + 1) * span] for ref in refs[:-1]]
        rows_ref[q * size : (q + 1) * size, :] = jnp.concatenate(found, axis=1)


def packed_trace(rows, batches, pack, size):
    groups = rows.shape[0] // (pack * size)
    return pl.pallas_call(
        pack_kernel,
        grid=(groups,),
        in_specs=[pl.BlockSpec((pack * size, rows.shape[1]), lambda i: (i, 0))],
        out_specs=pl.BlockSpec((batches, 1, size, LANES), lambda i: (0, i, 0, 0)),
        out_shape=jax.ShapeDtypeStruct((batches, groups, size, LANES), rows.dtype),
        compiler_params=pltpu.CompilerParams(vmem_limit_bytes=VMEM_BYTES),
        name="pack_trace",
    )(rows)


def unpacked_trace(packed, pack):
    groups, size, lanes = packed[0].shape
    columns = len(packed) * (lanes // pack)
    return pl.pallas_call(
        unpack_kernel,
        grid=(groups,),
        in_specs=[pl.BlockSpec((1, size, lanes), lambda i: (i, 0, 0))] * len(packed),
        out_specs=pl.BlockSpec((pack * size, columns), lambda i: (i, 0)),
        out_shape=jax.ShapeDtypeStruct((groups * pack * size, columns), jnp.float32),
        compiler_params=pltpu.CompilerParams(vmem_limit_bytes=VMEM_BYTES),
        name="unpack_trace",
    )(*packed)


def in_hbm(array):
    return pltpu.with_memory_space_constraint(array, pltpu.HBM)


def half_kernel(place_ref, values_ref, *refs):
    refs[-1][...] = values_ref[...]


def other_half(values, place, after):
    rows = values.shape[0] // 2
    step = divisor_up_to(rows, 3)
    block = (step,) + values.shape[1:]
    spec = pltpu.PrefetchScalarGridSpec(
        num_scalar_prefetch=1,
        grid=(rows // step,),
        in_specs=[
            pl.BlockSpec(block, lambda i, place_ref: ((1 - place_ref[0]) * (rows // step) + i, 0, 0, 0)),
            pl.BlockSpec(memory_space=pl.ANY),
        ],
        out_specs=pl.BlockSpec(block, lambda i, place_ref: (i, 0, 0, 0)),
    )
    return pl.pallas_call(
        half_kernel,
        grid_spec=spec,
        out_shape=jax.ShapeDtypeStruct((rows,) + values.shape[1:], values.dtype),
        compiler_params=pltpu.CompilerParams(vmem_limit_bytes=VMEM_BYTES),
        name="other_half",
    )(place, values, after)


def split_kernel(place_ref, own_ref, other_ref, *refs):
    parts_ref = refs[-1]
    picks, size = own_ref.shape[1:3]
    for start, values_ref in ((0, own_ref), (picks, other_ref)):
        for k in range(picks):
            value = values_ref[0, k]
            high = value.astype(jnp.bfloat16)
            parts_ref[0, start + k, :size] = high
            parts_ref[0, start + k, size:] = (value - high.astype(jnp.float32)).astype(jnp.bfloat16)


def split_operator(values, other, place, after):
    _, picks, size, depth = values.shape
    rows = other.shape[0]
    spec = pltpu.PrefetchScalarGridSpec(
        num_scalar_prefetch=1,
        grid=(rows,),
        in_specs=[
            pl.BlockSpec((1, picks, size, depth), lambda i, place_ref: (place_ref[0] * rows + i, 0, 0, 0)),
            pl.BlockSpec((1, picks, size, depth), lambda i, place_ref: (i, 0, 0, 0)),
            pl.BlockSpec(memory_space=pltpu.HBM),
        ],
        out_specs=pl.BlockSpec((1, 2 * picks, 2 * size, depth), lambda i, place_ref: (i, 0, 0, 0)),
    )
    return pl.pallas_call(
        split_kernel,
        grid_spec=spec,
        out_shape=jax.ShapeDtypeStruct((rows, 2 * picks, 2 * size, depth), jnp.bfloat16),
        compiler_params=pltpu.CompilerParams(vmem_limit_bytes=VMEM_BYTES),
        name="split_operator",
    )(place, values, other, in_hbm(after))


def apply_kernel(pack, index_ref, parts_ref, own_ref, other_ref, *refs):
    result_ref, token_ref, slots, tiles, arrived = refs[-5:]
    row, rows = pl.program_id(0), pl.num_programs(0)
    count, picks, twice, _ = slots.shape
    size = twice // 2
    pieces, groups, _, lanes = own_ref.shape
    span = lanes // pack

    def fetch(which):
        slot = lax.rem(which, count)
        return pltpu.make_async_copy(parts_ref.at[which], slots.at[slot], arrived.at[slot])

    @pl.when(row == 0)
    def _():
        for ahead in range(min(count - 1, parts_ref.shape[0])):
            fetch(ahead).start()

    @pl.when(row + count - 1 < rows)
    def _():
        fetch(row + count - 1).start()

    @pl.when(row == 0)
    def _():
        token_ref[...] = jnp.zeros_like(token_ref)
        middle = lanes // 2
        lane = lax.broadcasted_iota(jnp.int32, (size, lanes), 1) // span % max(1, pack // 2)
        masks = [(lane == q).astype(jnp.float32).astype(jnp.bfloat16) for q in range(pack // 2)]
        for half, ref in enumerate((own_ref, other_ref)):
            for piece in range(pieces):
                for group in range(groups):
                    tile = ref[piece, group]
                    high = tile.astype(jnp.bfloat16)
                    low = (tile - high.astype(jnp.float32)).astype(jnp.bfloat16)
                    base = ((half * pieces + piece) * groups + group) * pack
                    if pack == 1:
                        tiles[base] = jnp.concatenate([high, low], axis=1)
                        continue
                    first = jnp.concatenate([high[:, :middle], low[:, :middle]], axis=1)
                    second = jnp.concatenate([high[:, middle:], low[:, middle:]], axis=1)
                    for start, both in ((base, first), (base + pack // 2, second)):
                        for q, mask in enumerate(masks):
                            tiles[start + q] = both if pack == 2 else both * mask

    fetch(row).wait()
    slot = lax.rem(row, count)
    picked = jnp.concatenate([tiles[index_ref[row * picks + k]] for k in range(picks)], axis=0)
    block = jnp.concatenate([slots[slot, k] for k in range(picks)], axis=1)
    product = jnp.dot(block, picked, preferred_element_type=jnp.float32)
    total = product[:size] + product[size:]
    if pack == 1:
        result_ref[0] = total[:, :lanes] + total[:, lanes:]
    else:
        shift = span
        while shift < lanes:
            total = total + pltpu.roll(total, shift, 1)
            shift *= 2
        lane = lax.broadcasted_iota(jnp.int32, total.shape, 1)
        result_ref[0] = jnp.where(lane < lax.rem(row, pack) * span, result_ref[0], total)


def apply_operator(parts, index, pack, gathered, after):
    rows, picks, twice, depth = parts.shape
    pieces, groups, size, lanes = gathered[0].shape
    whole = pl.BlockSpec(gathered[0].shape, lambda row, *_: (0, 0, 0, 0))
    spec = pltpu.PrefetchScalarGridSpec(
        num_scalar_prefetch=1,
        grid=(rows,),
        in_specs=[
            pl.BlockSpec(memory_space=pltpu.HBM),
            whole,
            whole,
        ]
        + [pl.BlockSpec(memory_space=pl.ANY)] * len(after),
        out_specs=[pl.BlockSpec((1, size, lanes), lambda row, *_: (row // pack, 0, 0)), TOKEN_SPEC],
        scratch_shapes=[
            pltpu.VMEM((SLOTS, picks, twice, depth), jnp.bfloat16),
            pltpu.VMEM((2 * pieces * groups * pack, size, lanes * (2 if pack == 1 else 1)), jnp.bfloat16),
            pltpu.SemaphoreType.DMA((SLOTS,)),
        ],
    )

    def kernel(*refs):
        apply_kernel(pack, *refs)

    return pl.pallas_call(
        kernel,
        grid_spec=spec,
        out_shape=[jax.ShapeDtypeStruct((groups, size, lanes), jnp.float32), TOKEN],
        compiler_params=pltpu.CompilerParams(vmem_limit_bytes=VMEM_BYTES),
        cost_estimate=pl.CostEstimate(flops=0, bytes_accessed=gathered[0].size, transcendentals=0),
        name="apply_operator",
    )(index, in_hbm(parts), *gathered, *after)


def sum_kernel(terms, *refs):
    total_ref, token_ref = refs[-2:]
    total_ref[...] = sum(ref[...] for ref in refs[:terms])
    token_ref[...] = jnp.zeros_like(token_ref)


def sum_of(terms, after):
    shape = terms[0].shape
    whole = pl.BlockSpec(shape, lambda i: (0, 0, 0))

    def kernel(*refs):
        sum_kernel(len(terms), *refs)

    return pl.pallas_call(
        kernel,
        grid=(1,),
        in_specs=[whole] * len(terms) + [pl.BlockSpec(memory_space=pl.ANY)] * len(after),
        out_specs=[whole, TOKEN_SPEC],
        out_shape=[jax.ShapeDtypeStruct(shape, jnp.float32), TOKEN],
        compiler_params=pltpu.CompilerParams(vmem_limit_bytes=VMEM_BYTES),
        name="sum_of",
    )(*terms, *after)


def shards(sources, tr_vals, tr_cols, rf_vals, rf_cols):
    source = sources[0, 0, 0]
    piece_rows, columns = source.shape
    size = tr_vals.shape[-1]
    blocks = piece_rows // size
    pack = 2 if blocks % 2 == 0 else 1
    batches, delay = columns // (LANES // pack), DELAY
    length, pieces = lax.axis_size("slab"), lax.axis_size("col")
    last = length - 1
    position = lax.axis_index("slab")
    place = lax.axis_index("row")
    swap = [(0, 1), (1, 0)]
    source = packed_trace(source, batches, pack, size)

    def operator(values, columns, copy_after, split_after):
        half = values.shape[0] // 2
        own = lax.dynamic_slice_in_dim(columns, place * half, half, 0)
        other = lax.dynamic_slice_in_dim(columns, (1 - place) * half, half, 0)
        group_blocks = pieces * blocks
        index = jnp.concatenate([own, lax.ppermute(other, "row", swap) + group_blocks], axis=1)
        traded = lax.ppermute(other_half(values, place.reshape(1), copy_after), "row", swap)
        return split_operator(values, traded, place.reshape(1), split_after), index.reshape(-1), pack

    def by_position(choices):
        known = [choice for choice in choices if choice is not None]
        chosen = known[-1]
        for slab, choice in enumerate(choices):
            if choice is not None and choice is not chosen:
                chosen = jnp.where(position == slab, choice, chosen)
        return chosen

    def held(results, batch_of, shift):
        return by_position(
            [
                results[batch_of(slab) + shift(slab)] if 0 <= batch_of(slab) < batches else None
                for slab in range(length)
            ]
        )

    def gather(piece):
        gathered = lax.all_gather(piece, "col", axis=0)
        return gathered, lax.ppermute(gathered, "row", swap)

    moments = batches + delay * last
    downs, refls, ups, tokens = [], [], [], []

    def incident_of(moment, ready=()):
        after = [*tokens[moment - delay : moment - delay + 1], *ready]
        if moment < moments:
            which = jnp.clip(moment - delay * position, 0, batches - 1)
            terms = [lax.dynamic_index_in_dim(source, which, 0, keepdims=False)]
            if moment >= delay:
                terms.append(passed_along(downs[moment - delay], "slab", 1))
        else:
            at = moment - moments
            terms = [held(refls, lambda slab: at - delay * (last - slab), lambda slab: delay * slab)]
            if at >= delay:
                terms.append(passed_along(ups[at - delay], "slab", -1))
        return sum_of(terms, after)

    piece, _ = incident_of(0)
    gathered = [gather(piece)]
    trans = operator(tr_vals[0, 0, 0], tr_cols[0, 0, 0], piece, gathered[0][0])
    lag = max(0, min(delay, batches - 2))
    copied_after, ready = piece, []
    for moment in range(2 * moments):
        after = tokens[-1:]
        if moment + 1 < 2 * moments:
            piece, token = incident_of(moment + 1, ready if moment == lag else [])
            gathered.append(gather(piece))
            after = after + [token]
        product, token = apply_operator(*trans, gathered[moment], after)
        (downs if moment < moments else ups).append(product)
        if moment == max(0, lag - 1):
            refl = operator(rf_vals[0, 0, 0], rf_cols[0, 0, 0], copied_after, token)
            ready = [in_hbm(refl[0])]
        if lag <= moment < moments + lag:
            product, token = apply_operator(*refl, gathered[moment - lag], [token])
            refls.append(product)
        tokens.append(token)
    totals = [
        held(downs, lambda slab: batch, lambda slab: delay * slab)
        + held(ups, lambda slab: batch, lambda slab: delay * (last - slab))
        for batch in range(batches)
    ]
    return unpacked_trace(totals, pack)[None, None, None]


def solution(mesh):
    placed = (
        P("slab", "col", "row", None, None),
        P("slab", "col", "row", None, None, None, None),
        P("slab", "col", "row", None, None),
        P("slab", "col", "row", None, None, None, None),
        P("slab", "col", "row", None, None),
    )
    return jax.shard_map(
        shards,
        mesh=mesh,
        in_specs=placed,
        out_specs=P("slab", "col", "row", None, None),
        check_vma=False,
    )
```
